512 devices in a mesh: grp: 16 (over y, core), dev: 32 (over x, z).
Axes of the slice: x: 4, y: 8, z: 8, core: 2. Of those that a mesh axis runs over, the one named last changes fastest.
Arguments:
- forcing: float32 [8, 8, 8, 32, 16, 128], P(None, None, None, 'dev', 'grp'), may hold values from -6 to 6
- coefficient: float32 [32, 16, 128], P('dev', 'grp'), may hold values from 1 to 10
- coarse_inverse: float32 [16384, 1024], P(('grp', 'dev')), as said below
Outputs:
- solution: float32 [8, 8, 8, 32, 16, 128], P(None, None, None, 'dev', 'grp')
- residual: float32 [8, 8, 8, 32, 16, 128], P(None, None, None, 'dev', 'grp')
The draws below stay inside these ranges and needn't reach their ends.
Inputs may be any that keep to these rules, and one draw needn't show every extreme that they name: Each group's block of coarse_inverse is symmetric and positive definite.
All inputs are finite; a program needn't handle non-finite values.
Results may differ from the reference program's by a relative error of at most 0.017.
Values sent between devices are 32-bit elements; how exact they have to be, the bound alone decides.
A program may use at most 64 MiB of HBM per device.

```python
import math
import jax
import jax.numpy as jnp
from jax import lax

NP = 8
EZ = 128
NC_DEV = 32
ITERS = 2
AGG = 4
NC = 1024
GX = 32
GY = 16
N_GRP = 16
N_DEV = 32


def draw_coarse_inverse(key, part):
    key = jax.random.fold_in(key, 11)
    key_off, key_diag = jax.random.split(key)
    raw = jax.random.normal(key_off, (GY, NC, NC), jnp.float32)
    symmetric = (raw + jnp.swapaxes(raw, 1, 2)) * (0.17 / math.sqrt(NC))
    diagonal = jnp.exp(jax.random.uniform(key_diag, (GY, NC), jnp.float32, math.log(1.5), math.log(3.0)))
    unknown_ids = jnp.arange(NC)
    partner = (unknown_ids // NC_DEV + GX // 2) % GX * NC_DEV + unknown_ids % NC_DEV
    paired = (partner[:, None] == unknown_ids[None, :]).astype(jnp.float32)
    identity = jnp.eye(NC, dtype=jnp.float32)
    off_part = symmetric * (1.0 - identity) * (1.0 - paired) + 0.7 * paired
    full = 12.0 * (off_part + identity * diagonal[:, :, None])
    return full.reshape(GY * NC, NC)


def levels(rng, dims, cuts, low, top_value):
    loudness, own = 1.0, jax.random.fold_in(rng, 6)
    for dim, shards_of in cuts:
        heights = jnp.exp(jax.random.uniform(jax.random.fold_in(own, dim), (shards_of,), jnp.float32, low / len(cuts), top_value / len(cuts)))
        loudness = loudness * jnp.repeat(heights, dims[dim] // shards_of).reshape([-1 if axis == dim else 1 for axis in range(len(dims))])
    return loudness


def noise(rng, extent, deviation, limit, shards=(), kind=jnp.bfloat16):
    result = jax.random.normal(rng, extent, jnp.float32) * deviation
    if len(shards) > 0:
        result = levels(rng, extent, shards, -0.22, 0.18) * result
    return jnp.clip(result, min=-limit, max=limit).astype(kind)


def setup_inputs(seed: int = 0) -> dict:
    keys = jax.random.split(jax.random.key(seed), 4)
    forcing = noise(keys[0], (NP, NP, NP, GX, GY, EZ), 1.0, 6.0, ((3, 32), (4, 16)), jnp.float32)
    coefficient = jnp.clip(jnp.exp(math.log(10.0) - 2.3025851 * jax.random.uniform(keys[1], (GX, GY, EZ), jnp.float32) ** levels(keys[1], (GX, GY, EZ), ((0, 32), (1, 16)), -0.2, 0.2)), 1.0, 10.0)
    coarse_inverse = draw_coarse_inverse(jax.random.fold_in(keys[3], 71), 0)
    return dict(forcing=forcing, coefficient=coefficient, coarse_inverse=coarse_inverse)


HIGHEST = lax.Precision.HIGHEST
MASS_SHIFT = 0.1

def legendre_pair(order, point):
    before = 1.0
    current = point
    for degree in range(2, order + 1):
        before, current = (current, ((2 * degree - 1) * point * current - (degree - 1) * before) / degree)
    return (before, current)

def jacobi_eigen(matrix_in):
    count = len(matrix_in)
    work = [list(row_vals) for row_vals in matrix_in]
    vectors = [[1.0 if row_id == col_id else 0.0 for col_id in range(count)] for row_id in range(count)]
    for sweep_id in range(14):
        for first_id in range(count - 1):
            for second_id in range(first_id + 1, count):
                off_value = work[first_id][second_id]
                if abs(off_value) > 1e-300:
                    theta = (work[second_id][second_id] - work[first_id][first_id]) / (2.0 * off_value)
                    sign_val = 1.0 if theta >= 0.0 else -1.0
                    tangent = sign_val / (abs(theta) + math.sqrt(theta * theta + 1.0))
                    cosine = 1.0 / math.sqrt(tangent * tangent + 1.0)
                    sine = tangent * cosine
                    for other_id in range(count):
                        left_val = work[other_id][first_id]
                        right_val = work[other_id][second_id]
                        work[other_id][first_id] = cosine * left_val - sine * right_val
                        work[other_id][second_id] = sine * left_val + cosine * right_val
                    for other_id in range(count):
                        left_val = work[first_id][other_id]
                        right_val = work[second_id][other_id]
                        work[first_id][other_id] = cosine * left_val - sine * right_val
                        work[second_id][other_id] = sine * left_val + cosine * right_val
                    for other_id in range(count):
                        left_val = vectors[other_id][first_id]
                        right_val = vectors[other_id][second_id]
                        vectors[other_id][first_id] = cosine * left_val - sine * right_val
                        vectors[other_id][second_id] = sine * left_val + cosine * right_val
    return ([work[idx_val][idx_val] for idx_val in range(count)], vectors)

def element_tables(point_count):
    poly_order = point_count - 1
    points = [-math.cos(math.pi * idx_val / poly_order) for idx_val in range(point_count)]
    for newton_id in range(100):
        updated = []
        for point in points:
            before, current = legendre_pair(poly_order, point)
            updated.append(point - (point * current - before) / (point_count * current))
        points = updated
    values = [legendre_pair(poly_order, point)[1] for point in points]
    weights = [2.0 / (poly_order * point_count * value ** 2) for value in values]
    derivative = [[0.0] * point_count for row_id in range(point_count)]
    for left_index in range(point_count):
        for right_index in range(point_count):
            if left_index != right_index:
                derivative[left_index][right_index] = values[left_index] / (values[right_index] * (points[left_index] - points[right_index]))
    derivative[0][0] = -poly_order * point_count / 4.0
    derivative[poly_order][poly_order] = poly_order * point_count / 4.0
    stiffness = [[sum((derivative[inner_id][row_id] * weights[inner_id] * derivative[inner_id][col_id] for inner_id in range(point_count))) for col_id in range(point_count)] for row_id in range(point_count)]
    size_three = 3 * poly_order + 1
    stiff_three = [[0.0] * size_three for row_id in range(size_three)]
    mass_three = [0.0] * size_three
    for element in range(3):
        first_node = element * poly_order
        for row_id in range(point_count):
            mass_three[first_node + row_id] += weights[row_id]
            for col_id in range(point_count):
                stiff_three[first_node + row_id][first_node + col_id] += stiffness[row_id][col_id]
    keep = list(range(poly_order - 1, 2 * poly_order + 2))
    scale_half = [1.0 / math.sqrt(mass_three[idx_val]) for idx_val in keep]
    scaled = [[scale_half[row_id] * stiff_three[keep[row_id]][keep[col_id]] * scale_half[col_id] for col_id in range(len(keep))] for row_id in range(len(keep))]
    eigen_values, vectors = jacobi_eigen(scaled)
    transform = [[scale_half[row_id] * vectors[row_id][col_id] for col_id in range(len(keep))] for row_id in range(len(keep))]
    return (weights, stiffness, eigen_values, transform)

def device_tables():
    tables = element_tables(NP)
    return tuple((jnp.asarray(table, dtype=jnp.float32) for table in tables))

def tensor_apply(matrix, tensor, node_axis):
    patterns = ('ai,ijkxyz->ajkxyz', 'aj,ijkxyz->iakxyz', 'ak,ijkxyz->ijaxyz')
    return jnp.einsum(patterns[node_axis], matrix, tensor, precision=HIGHEST)

def cut_out(tensor, begin_at, end_at, node_axis):
    return lax.slice_in_dim(tensor, begin_at, end_at, axis=node_axis)

def shift_elements(tensor, elem_axis, forward, periodic):
    elem_count = tensor.shape[elem_axis]
    if forward:
        incoming = cut_out(tensor, elem_count - 1, elem_count, elem_axis)
        if not periodic:
            incoming = jnp.zeros_like(incoming)
        return jnp.concatenate([incoming, cut_out(tensor, 0, elem_count - 1, elem_axis)], axis=elem_axis)
    incoming = cut_out(tensor, 0, 1, elem_axis)
    if not periodic:
        incoming = jnp.zeros_like(incoming)
    return jnp.concatenate([cut_out(tensor, 1, elem_count, elem_axis), incoming], axis=elem_axis)

def assemble(vector):
    for node_axis, periodic in ((0, True), (1, False), (2, True)):
        elem_axis = node_axis + 3
        low_face = cut_out(vector, 0, 1, node_axis)
        high_face = cut_out(vector, NP - 1, NP, node_axis)
        new_low = low_face + shift_elements(high_face, elem_axis, True, periodic)
        new_high = high_face + shift_elements(low_face, elem_axis, False, periodic)
        vector = jnp.concatenate([new_low, cut_out(vector, 1, NP - 1, node_axis), new_high], axis=node_axis)
    return vector

def mass_cube(weights):
    cube = weights[:, None, None] * weights[None, :, None] * weights[None, None, :]
    return cube[:, :, :, None, None, None]

def local_operator(vector, coefficient, weights, stiffness):
    weight_x = weights.reshape(NP, 1, 1, 1, 1, 1)
    weight_y = weights.reshape(1, NP, 1, 1, 1, 1)
    weight_z = weights.reshape(1, 1, NP, 1, 1, 1)
    stiff_term = tensor_apply(stiffness, vector, 0) * weight_y * weight_z
    stiff_term = stiff_term + tensor_apply(stiffness, vector, 1) * weight_x * weight_z
    stiff_term = stiff_term + tensor_apply(stiffness, vector, 2) * weight_x * weight_y
    return coefficient[None, None, None] * stiff_term + MASS_SHIFT * weight_x * weight_y * weight_z * vector

def extend(vector):
    for node_axis, periodic in ((0, True), (1, False), (2, True)):
        elem_axis = node_axis + 3
        inner_low = cut_out(vector, 1, 2, node_axis)
        inner_high = cut_out(vector, NP - 2, NP - 1, node_axis)
        vector = jnp.concatenate([shift_elements(inner_high, elem_axis, True, periodic), vector, shift_elements(inner_low, elem_axis, False, periodic)], axis=node_axis)
    return vector

def local_solve(extended, coefficient, eigen_values, transform):
    tensor = tensor_apply(transform.T, extended, 0)
    tensor = tensor_apply(transform.T, tensor, 1)
    tensor = tensor_apply(transform.T, tensor, 2)
    eigen_sum = eigen_values[:, None, None] + eigen_values[None, :, None] + eigen_values[None, None, :]
    tensor = tensor / (coefficient[None, None, None] * eigen_sum[:, :, :, None, None, None] + MASS_SHIFT)
    tensor = tensor_apply(transform, tensor, 0)
    tensor = tensor_apply(transform, tensor, 1)
    return tensor_apply(transform, tensor, 2)

def fold(solved):
    for node_axis, periodic in ((2, True), (1, False), (0, True)):
        elem_axis = node_axis + 3
        first_layer = cut_out(solved, 0, 1, node_axis)
        last_layer = cut_out(solved, NP + 1, NP + 2, node_axis)
        middle = cut_out(solved, 1, NP + 1, node_axis)
        add_one = shift_elements(last_layer, elem_axis, True, periodic)
        add_six = shift_elements(first_layer, elem_axis, False, periodic)
        solved = jnp.concatenate([cut_out(middle, 0, 1, node_axis), cut_out(middle, 1, 2, node_axis) + add_one, cut_out(middle, 2, NP - 2, node_axis), cut_out(middle, NP - 2, NP - 1, node_axis) + add_six, cut_out(middle, NP - 1, NP, node_axis)], axis=node_axis)
    return solved

def precondition(residual, coefficient, coarse_inverse, tables):
    weights, stiffness, eigen_values, transform = tables
    solved = fold(local_solve(extend(residual), coefficient, eigen_values, transform))
    cube = mass_cube(weights)
    element_sums = lax.optimization_barrier(jnp.sum(cube * residual, axis=(0, 1, 2)))
    grouped = element_sums.reshape(N_DEV, N_GRP, NC_DEV, AGG).sum(axis=3)
    coarse_res = jnp.transpose(grouped, (1, 0, 2)).reshape(N_GRP, NC)
    blocks = coarse_inverse.reshape(N_GRP, NC, NC)
    coarse_sol = jnp.einsum('gab,gb->ga', blocks, coarse_res, precision=HIGHEST)
    spread = jnp.transpose(coarse_sol.reshape(N_GRP, N_DEV, NC_DEV), (1, 0, 2))
    spread = jnp.broadcast_to(spread[:, :, :, None], (N_DEV, N_GRP, NC_DEV, AGG)).reshape(N_DEV, N_GRP, EZ)
    return assemble(solved + cube * spread[None, None, None])

def inverse_multiplicity(first_row, total_rows, rows_here):
    layer_ids = jnp.arange(NP)
    shared = (layer_ids == 0) | (layer_ids == NP - 1)
    plain_mult = jnp.where(shared, 2.0, 1.0).astype(jnp.float32)
    row_ids = first_row + jnp.arange(rows_here)
    at_wall = (layer_ids[:, None] == 0) & (row_ids[None, :] == 0) | (layer_ids[:, None] == NP - 1) & (row_ids[None, :] == total_rows - 1)
    row_mult = jnp.where(shared[:, None] & jnp.logical_not(at_wall), 2.0, 1.0).astype(jnp.float32)
    multiplicity = plain_mult.reshape(NP, 1, 1, 1, 1, 1) * row_mult.reshape(1, NP, 1, 1, rows_here, 1) * plain_mult.reshape(1, 1, NP, 1, 1, 1)
    return 1.0 / multiplicity

def reference(forcing, coefficient, coarse_inverse):
    tables = device_tables()
    weights, stiffness = (tables[0], tables[1])
    inverse_mult = inverse_multiplicity(0, N_GRP, N_GRP)

    def inner_product(left_vec, right_vec):
        return jnp.sum(left_vec * right_vec * inverse_mult)

    def apply_operator(vector):
        return assemble(local_operator(vector, coefficient, weights, stiffness))
    load = assemble(forcing)
    solution = jnp.zeros_like(load)
    residual = load
    precond = precondition(residual, coefficient, coarse_inverse, tables)
    direction = precond
    gamma_now = inner_product(residual, precond)
    for iteration in range(ITERS):
        image = apply_operator(direction)
        step_len = gamma_now / inner_product(direction, image)
        solution = solution + step_len * direction
        residual = residual - step_len * image
        if iteration + 1 < ITERS:
            precond = precondition(residual, coefficient, coarse_inverse, tables)
            gamma_next = inner_product(residual, precond)
            direction = precond + gamma_next / gamma_now * direction
            gamma_now = gamma_next
    return (solution, residual)
```

```python
import functools
import math

import jax
import jax.numpy as jnp
import ml_dtypes
import numpy as np
from jax import lax
from jax.experimental import pallas as pl
from jax.experimental.pallas import tpu as pltpu
from jax.sharding import PartitionSpec as P

NP = 8
NX = NP + 2
LANES = 128
MASS_SHIFT = 0.1
HIGHEST = lax.Precision.HIGHEST


def legendre_pair(order, point):
    before = 1.0
    current = point
    for degree in range(2, order + 1):
        before, current = (
            current,
            ((2 * degree - 1) * point * current - (degree - 1) * before) / degree,
        )
    return (before, current)


def jacobi_eigen(matrix_in):
    count = len(matrix_in)
    work = [list(row_vals) for row_vals in matrix_in]
    vectors = [
        [1.0 if row_id == col_id else 0.0 for col_id in range(count)] for row_id in range(count)
    ]
    for sweep_id in range(14):
        for first_id in range(count - 1):
            for second_id in range(first_id + 1, count):
                off_value = work[first_id][second_id]
                if abs(off_value) > 1e-300:
                    theta = (work[second_id][second_id] - work[first_id][first_id]) / (
                        2.0 * off_value
                    )
                    sign_val = 1.0 if theta >= 0.0 else -1.0
                    tangent = sign_val / (abs(theta) + math.sqrt(theta * theta + 1.0))
                    cosine = 1.0 / math.sqrt(tangent * tangent + 1.0)
                    sine = tangent * cosine
                    for other_id in range(count):
                        left_val = work[other_id][first_id]
                        right_val = work[other_id][second_id]
                        work[other_id][first_id] = cosine * left_val - sine * right_val
                        work[other_id][second_id] = sine * left_val + cosine * right_val
                    for other_id in range(count):
                        left_val = work[first_id][other_id]
                        right_val = work[second_id][other_id]
                        work[first_id][other_id] = cosine * left_val - sine * right_val
                        work[second_id][other_id] = sine * left_val + cosine * right_val
                    for other_id in range(count):
                        left_val = vectors[other_id][first_id]
                        right_val = vectors[other_id][second_id]
                        vectors[other_id][first_id] = cosine * left_val - sine * right_val
                        vectors[other_id][second_id] = sine * left_val + cosine * right_val
    return ([work[idx_val][idx_val] for idx_val in range(count)], vectors)


def element_tables(point_count):
    poly_order = point_count - 1
    points = [-math.cos(math.pi * idx_val / poly_order) for idx_val in range(point_count)]
    for newton_id in range(100):
        updated = []
        for point in points:
            before, current = legendre_pair(poly_order, point)
            updated.append(point - (point * current - before) / (point_count * current))
        points = updated
    values = [legendre_pair(poly_order, point)[1] for point in points]
    weights = [2.0 / (poly_order * point_count * value**2) for value in values]
    derivative = [[0.0] * point_count for row_id in range(point_count)]
    for left_index in range(point_count):
        for right_index in range(point_count):
            if left_index != right_index:
                derivative[left_index][right_index] = values[left_index] / (
                    values[right_index] * (points[left_index] - points[right_index])
                )
    derivative[0][0] = -poly_order * point_count / 4.0
    derivative[poly_order][poly_order] = poly_order * point_count / 4.0
    stiffness = [
        [
            sum(
                (
                    derivative[inner_id][row_id] * weights[inner_id] * derivative[inner_id][col_id]
                    for inner_id in range(point_count)
                )
            )
            for col_id in range(point_count)
        ]
        for row_id in range(point_count)
    ]
    size_three = 3 * poly_order + 1
    stiff_three = [[0.0] * size_three for row_id in range(size_three)]
    mass_three = [0.0] * size_three
    for element in range(3):
        first_node = element * poly_order
        for row_id in range(point_count):
            mass_three[first_node + row_id] += weights[row_id]
            for col_id in range(point_count):
                stiff_three[first_node + row_id][first_node + col_id] += stiffness[row_id][col_id]
    keep = list(range(poly_order - 1, 2 * poly_order + 2))
    scale_half = [1.0 / math.sqrt(mass_three[idx_val]) for idx_val in keep]
    scaled = [
        [
            scale_half[row_id] * stiff_three[keep[row_id]][keep[col_id]] * scale_half[col_id]
            for col_id in range(len(keep))
        ]
        for row_id in range(len(keep))
    ]
    eigen_values, vectors = jacobi_eigen(scaled)
    transform = [
        [scale_half[row_id] * vectors[row_id][col_id] for col_id in range(len(keep))]
        for row_id in range(len(keep))
    ]
    return (weights, stiffness, eigen_values, transform)


KROWS = 112
PAIRS = ((0, 1), (8, 9), (2, 3), (4, 5), (6, 7))
SIDES = ((1, 0), (-1, 0), (0, 1), (0, -1), (1, 1), (1, -1), (-1, 1), (-1, -1))


def split_bf16(matrix):
    high = matrix.astype(ml_dtypes.bfloat16)
    low = (matrix - high.astype(np.float64)).astype(ml_dtypes.bfloat16)
    return high, low


def stacked(matrix):
    high, low = split_bf16(matrix)
    return np.concatenate(
        [np.concatenate([high, high], 1), np.concatenate([low, np.zeros_like(low)], 1)], 0
    )


@functools.lru_cache(maxsize=None)
def constants():
    weights, stiffness, eigen_values, transform = (
        np.array(table, dtype=np.float64) for table in element_tables(NP)
    )
    forward = np.zeros((KROWS, KROWS))
    lam_rows = np.zeros((KROWS,))
    for b in range(NX):
        for c in range(NX):
            row = b * NX + c
            lam_rows[row] = eigen_values[b] + eigen_values[c]
            for j in range(NX):
                for k in range(NX):
                    if k == 0:
                        col = 80 + j
                    elif k == NX - 1:
                        col = 96 + j
                    else:
                        col = j * NP + k - 1
                    forward[row, col] = transform[j, b] * transform[k, c]
    diag_w = np.diag(weights)
    plane = np.kron(stiffness, diag_w) + np.kron(diag_w, stiffness)
    table = np.zeros((128, LANES), np.float32)
    table[:KROWS] = lam_rows[:, None]
    table[KROWS : KROWS + NP] = weights[:, None]
    half = np.ones((NP,))
    half[0] = half[-1] = 0.5
    table[KROWS + NP :] = half[:, None]
    return dict(
        weights=[float(v) for v in weights],
        stiffness=stiffness,
        eigen=[float(v) for v in eigen_values],
        transform=transform,
        forward=stacked(forward),
        back=stacked(forward.T),
        plane=stacked(plane),
        table=table,
    )


def combine(scalars, vectors):
    total = None
    for scalar, vector in zip(scalars, vectors):
        term = float(scalar) * vector
        total = term if total is None else total + term
    return total


def dot_split(matrix, value):
    rows = value.shape[0]
    high = value.astype(jnp.bfloat16)
    low = (value - high.astype(jnp.float32)).astype(jnp.bfloat16)
    out = jnp.dot(
        matrix, jnp.concatenate([high, low], axis=0), preferred_element_type=jnp.float32
    )
    return out[:rows] + out[rows:]


def lane_fold(value):
    value = value + pltpu.roll(value, 64, 1)
    return value + pltpu.roll(value, 32, 1)


def next_lane(value, axis):
    return pltpu.roll(value, LANES - 1, axis)


def previous_lane(value, axis):
    return pltpu.roll(value, 1, axis)


def face_range(step, low, middle, high):
    return {1: high, -1: low, 0: middle}[step]


EQ_X = (slice(0, 2), slice(0, 8), slice(6, 8))
EQ_Y = (slice(0, 16), slice(0, 64), slice(48, 64))
QF_X = (slice(0, 2), slice(1, 9), slice(8, 10))
QF_Y = (slice(0, 16), slice(8, 72), slice(64, 80))
Q_X = (slice(0, 1), slice(0, 8), slice(7, 8))
Q_Y = (slice(0, 8), slice(0, 64), slice(56, 64))


def kernel(
    n_grp,
    n_dev,
    f_ref,
    coef_ref,
    rows_ref,
    table_ref,
    fwd_ref,
    back_ref,
    plane_ref,
    sol_ref,
    res_ref,
    u0,
    u1,
    u2,
    e0,
    e1,
    s0,
    s1,
    z0,
    z1,
    work,
    inv_ref,
    x1,
    y1,
    c1,
    x2,
    y2,
    c2,
    x3,
    y3,
    c3,
    x4,
    y4,
    c4,
    x5,
    y5,
    c5,
    coarse_a,
    coarse_b,
    dots_a,
    dots_b,
    dots_c,
    dots_d,
    send_sem,
    recv_sem,
    bulk_send,
    bulk_recv,
):
    tabs = constants()
    weights = tabs["weights"]
    stiff = tabs["stiffness"]
    trans = tabs["transform"]
    eigen = tabs["eigen"]
    grp = lax.axis_index("grp")
    dev = lax.axis_index("dev")

    def dev_at(step):
        return lax.rem(dev + step + n_dev, n_dev)

    def grp_at(step):
        return lax.rem(grp + step + n_grp, n_grp)

    barrier = pltpu.get_barrier_semaphore()

    def greet_dev(step, carry):
        pl.semaphore_signal(
            barrier, inc=1, device_id=(grp, lax.rem(dev + step, n_dev)),
            device_id_type=pl.DeviceIdType.MESH,
        )
        return carry

    def greet_grp(step, carry):
        pl.semaphore_signal(
            barrier, inc=1, device_id=(lax.rem(grp + step, n_grp), dev),
            device_id_type=pl.DeviceIdType.MESH,
        )
        return carry

    lax.fori_loop(1, n_dev, greet_dev, 0)
    lax.fori_loop(1, n_grp, greet_grp, 0)
    for dx, dy in SIDES[4:]:
        pl.semaphore_signal(
            barrier, inc=1, device_id=(grp_at(dy), dev_at(dx)),
            device_id_type=pl.DeviceIdType.MESH,
        )

    def exchange(number, source, x_ranges, y_ranges, x_buf, y_buf, c_buf):
        copies = []
        for index, (dx, dy) in enumerate(SIDES):
            src = source.at[
                face_range(dx, *x_ranges), face_range(dy, *y_ranges), :
            ]
            if dy == 0:
                dst = x_buf.at[0 if dx == 1 else 1]
            elif dx == 0:
                dst = y_buf.at[0 if dy == 1 else 1]
            else:
                dst = c_buf.at[0 if dx == 1 else 1, 0 if dy == 1 else 1]
            copy = pltpu.make_async_remote_copy(
                src_ref=src,
                dst_ref=dst,
                send_sem=send_sem.at[number, index],
                recv_sem=recv_sem.at[number, index],
                device_id=(grp_at(dy), dev_at(dx)),
                device_id_type=pl.DeviceIdType.MESH,
            )
            copy.start()
            copies.append(copy)
        return copies

    def arrive(copies):
        for copy in copies:
            copy.wait_recv()

    def spread_row(buf, number, along_dev):
        count = n_dev if along_dev else n_grp
        me = dev if along_dev else grp

        def body(step, carry):
            other = lax.rem(me + step, count)
            pltpu.make_async_remote_copy(
                src_ref=buf.at[me],
                dst_ref=buf.at[me],
                send_sem=bulk_send.at[number],
                recv_sem=bulk_recv.at[number],
                device_id=(grp, other) if along_dev else (other, dev),
                device_id_type=pl.DeviceIdType.MESH,
            ).start()
            return carry

        lax.fori_loop(1, count, body, 0)

    def bulk_wait(buf, sem, count):
        part = buf.at[pl.ds(0, count - 1)]
        pltpu.make_async_copy(part, part, sem).wait()

    low_wall = jnp.where(grp == 0, 0.0, 1.0).astype(jnp.float32)
    high_wall = jnp.where(grp == n_grp - 1, 0.0, 1.0).astype(jnp.float32)
    coef = coef_ref[...]
    w_k = table_ref[KROWS : KROWS + NP, :]
    half_k = table_ref[KROWS + NP :, :]
    lane = lax.broadcasted_iota(jnp.int32, (1, LANES), 1)

    def assemble_z(ref):
        top = ref[:, pl.ds(0, NP, stride=NP), :]
        bottom = ref[:, pl.ds(NP - 1, NP, stride=NP), :]
        ref[:, pl.ds(0, NP, stride=NP), :] = top + previous_lane(bottom, 2)
        ref[:, pl.ds(NP - 1, NP, stride=NP), :] = bottom + next_lane(top, 2)

    u0[...] = f_ref[...]
    assemble_z(u0)
    pl.semaphore_wait(barrier, n_dev - 1 + n_grp - 1 + 4)
    round_1 = exchange(0, u0, EQ_X, EQ_Y, x1, y1, c1)

    lam_rows = table_ref[0:KROWS, :]
    for a in range(NX):
        inv_ref[a] = 1.0 / (coef * (lam_rows + eigen[a]) + MASS_SHIFT)
    zero_rows = jnp.zeros((128 - 80, LANES), jnp.float32)
    for i in range(NX):
        e0[i, 80:128, :] = zero_rows
        e1[i, 80:128, :] = zero_rows
        s0[i, 80:128, :] = zero_rows
        s1[i, 80:128, :] = zero_rows

    def extend_into(ext, own, x_buf, y_buf, c_buf):
        for i in range(NX):
            if i == 0:
                row = x_buf[0, 0]
                low = c_buf[0, 0, 0]
                high = c_buf[0, 1, 0]
            elif i == NX - 1:
                row = x_buf[1, 1]
                low = c_buf[1, 0, 1]
                high = c_buf[1, 1, 1]
            else:
                row = own[i - 1]
                low = y_buf[0, i - 1]
                high = y_buf[1, i - 1]
                if i == 1:
                    row = row + x_buf[0, 1]
                    low = low + c_buf[0, 0, 1]
                    high = high + c_buf[0, 1, 1]
                elif i == NX - 2:
                    row = row + x_buf[1, 0]
                    low = low + c_buf[1, 0, 0]
                    high = high + c_buf[1, 1, 0]
            low = low * low_wall
            high = high * high_wall
            ext[i, 0:8, :] = low[0:8]
            ext[i, 8:16, :] = row[0:8] + low[8:16]
            ext[i, 16:64, :] = row[8:56]
            ext[i, 64:72, :] = row[56:64] + high[0:8]
            ext[i, 72:80, :] = high[8:16]

    def start_coarse(ext, buf, number):
        total = None
        for i in range(NP):
            line = combine(
                weights, [ext[i + 1, 8 + NP * j : 16 + NP * j, :] for j in range(NP)]
            )
            total = weights[i] * line if total is None else total + weights[i] * line
        total = total * w_k
        elem = lax.broadcasted_iota(jnp.int32, (LANES, LANES), 0)
        place = lax.broadcasted_iota(jnp.int32, (LANES, LANES), 1)
        group = jnp.where(
            place == lax.rem(dev, 4) * 32 + lax.shift_right_logical(elem, 2), 1.0, 0.0
        ).astype(jnp.float32)
        sums = jnp.dot(total, group, precision=HIGHEST, preferred_element_type=jnp.float32)
        buf[dev] = jnp.sum(sums, axis=0, keepdims=True)
        spread_row(buf, number, True)

    def finish_coarse(buf, number):
        bulk_wait(buf, bulk_recv.at[number], n_dev)
        total = None
        for block in range(n_dev // 4):
            first = 4 * block
            row = (buf[first] + buf[first + 1]) + (buf[first + 2] + buf[first + 3])
            term = rows_ref[:, block * LANES : (block + 1) * LANES] * row
            total = term if total is None else total + term
        sums = jnp.sum(total, axis=1, keepdims=True)
        unknown = lax.broadcasted_iota(jnp.int32, (32, LANES), 0)
        elem = lax.broadcasted_iota(jnp.int32, (32, LANES), 1)
        mine = lax.shift_right_logical(elem, 2) == unknown
        sol = jnp.sum(jnp.where(mine, sums, 0.0), axis=0, keepdims=True)
        node = lax.broadcasted_iota(jnp.int32, (NP, LANES), 0)
        beside = jnp.where(node == 0, previous_lane(sol, 1), 0.0) + jnp.where(
            node == NP - 1, next_lane(sol, 1), 0.0
        )
        return w_k * (sol + beside)

    even = [a for a in range(NX) if abs(trans[0, a] - trans[9, a]) < abs(trans[0, a] + trans[9, a])]
    odd = [a for a in range(NX) if a not in even]

    def local_solve(ext, out):
        for pair in PAIRS:
            parts = []
            for i in pair:
                front = previous_lane(ext[i, pl.ds(6, 16, stride=NP), :], 1)
                behind = next_lane(ext[i, pl.ds(1, 16, stride=NP), :], 1)
                parts.append(jnp.concatenate([ext[i, 0:80, :], front, behind], axis=0))
            got = dot_split(fwd_ref[...], jnp.concatenate(parts, axis=1))
            work[pair[0]] = got[:, 0:LANES]
            work[pair[1]] = got[:, LANES:]

        def middle(block, carry):
            rows = pl.ds(pl.multiple_of(block * 8, 8), 8)
            vals = [work[i, rows, :] for i in range(NX)]
            plus = [vals[i] + vals[NX - 1 - i] for i in range(5)]
            minus = [vals[i] - vals[NX - 1 - i] for i in range(5)]
            modes = {}
            for a in range(NX):
                source = plus if a in even else minus
                modes[a] = combine(trans[:5, a], source) * inv_ref[a, rows, :]
            for i in range(5):
                sym = combine(trans[i, even], [modes[a] for a in even])
                anti = combine(trans[i, odd], [modes[a] for a in odd])
                work[i, rows, :] = sym + anti
                work[NX - 1 - i, rows, :] = sym - anti
            return carry

        lax.fori_loop(0, KROWS // 8, middle, 0)
        for pair in PAIRS:
            got = dot_split(
                back_ref[...], jnp.concatenate([work[pair[0]], work[pair[1]]], axis=1)
            )
            for side, i in enumerate(pair):
                part = got[:, side * LANES : (side + 1) * LANES]
                out[i, 0:80, :] = part[0:80]
                at_6 = pl.ds(6, 16, stride=NP)
                at_1 = pl.ds(1, 16, stride=NP)
                at_0 = pl.ds(0, 16, stride=NP)
                at_7 = pl.ds(7, 16, stride=NP)
                out[i, at_6, :] = out[i, at_6, :] + next_lane(part[80:96], 1)
                out[i, at_1, :] = out[i, at_1, :] + previous_lane(part[96:112], 1)
                top = out[i, at_0, :]
                bottom = out[i, at_7, :]
                out[i, at_0, :] = top + previous_lane(bottom, 1)
                out[i, at_7, :] = bottom + next_lane(top, 1)

    def add_coarse(out, coarse):
        for i in range(NP):
            for j in range(NP):
                rows = slice(8 + NP * j, 16 + NP * j)
                out[i + 1, rows, :] = out[i + 1, rows, :] + (weights[i] * weights[j]) * coarse

    def fold_field(out, i, x_buf, y_buf, c_buf):
        row = out[i + 1, 8:72, :]
        low = y_buf[0, i]
        high = y_buf[1, i]
        if i < 2:
            row = row + x_buf[0, i]
            low = low + c_buf[0, 0, i]
            high = high + c_buf[0, 1, i]
        elif i >= 6:
            row = row + x_buf[1, i - 6]
            low = low + c_buf[1, 0, i - 6]
            high = high + c_buf[1, 1, i - 6]
        return jnp.concatenate(
            [row[0:16] + low * low_wall, row[16:48], row[48:64] + high * high_wall], axis=0
        )

    def operate(field, out):
        total = jnp.zeros((NP, LANES), jnp.float32)
        for pair in ((0, 7), (1, 6), (2, 5), (3, 4)):
            got = dot_split(
                plane_ref[...], jnp.concatenate([field[pair[0]], field[pair[1]]], axis=1)
            )
            out[pair[0]] = got[:, 0:LANES]
            out[pair[1]] = got[:, LANES:]
        for j in range(NP):
            rows = slice(NP * j, NP * j + NP)
            vals = [field[i, rows, :] for i in range(NP)]
            plus = [vals[i] + vals[NP - 1 - i] for i in range(4)]
            minus = [vals[i] - vals[NP - 1 - i] for i in range(4)]
            w_yz = weights[j] * w_k
            coef_yz = coef * w_yz
            for i in range(4):
                sym = combine([(stiff[i, m] + stiff[i, 7 - m]) / 2 for m in range(4)], plus)
                anti = combine([(stiff[i, m] - stiff[i, 7 - m]) / 2 for m in range(4)], minus)
                for at, value in ((i, sym + anti), (7 - i, sym - anti)):
                    result = (
                        value * coef_yz
                        + (weights[at] * coef) * out[at, rows, :]
                        + (MASS_SHIFT * weights[at]) * (w_yz * vals[at])
                    )
                    out[at, rows, :] = result
                    total = total + result * vals[at]
        return total

    def inverse_mult(i, j):
        scale = 0.5 if i in (0, NP - 1) else 1.0
        if j == 0:
            return scale * (1.0 - 0.5 * low_wall)
        if j == NP - 1:
            return scale * (1.0 - 0.5 * high_wall)
        return scale

    def product(left, right):
        total = jnp.zeros((NP, LANES), jnp.float32)
        for j in range(NP):
            line = None
            for i in range(NP):
                term = left(i, j) * right(i, j)
                if i in (0, NP - 1):
                    term = 0.5 * term
                line = term if line is None else line + term
            if j == 0:
                line = line * (1.0 - 0.5 * low_wall)
            elif j == NP - 1:
                line = line * (1.0 - 0.5 * high_wall)
            total = total + line
        return total * half_k

    def from_ext(ext):
        return lambda i, j: ext[i + 1, 8 + NP * j : 16 + NP * j, :]

    def from_field(field):
        return lambda i, j: field[i, NP * j : NP * j + NP, :]

    def pack_dots(totals):
        packed = None
        for index, total in enumerate(totals):
            row = lane_fold(jnp.sum(total, axis=0, keepdims=True))
            mine = (lane >= 32 * index) & (lane < 32 * index + 32)
            row = jnp.where(mine, row, 0.0)
            packed = row if packed is None else packed + row
        return packed

    def unpack_dot(row, index):
        mine = (lane >= 32 * index) & (lane < 32 * index + 32)
        return jnp.sum(jnp.where(mine, row, 0.0), axis=1, keepdims=True)

    def add_slots(buf, count):
        rows = [buf[index] for index in range(count)]
        while len(rows) > 1:
            rows = [rows[index] + rows[index + 1] for index in range(0, len(rows), 2)]
        return rows[0]

    arrive(round_1)
    extend_into(e0, u0, x1, y1, c1)
    start_coarse(e0, coarse_a, 0)
    local_solve(e0, s0)
    add_coarse(s0, finish_coarse(coarse_a, 0))
    round_2 = exchange(1, s0, QF_X, QF_Y, x2, y2, c2)
    arrive(round_2)
    for i in range(NP):
        z0[i] = fold_field(s0, i, x2, y2, c2)

    delta_part = operate(z0, u1)
    assemble_z(u1)
    round_3 = exchange(2, u1, EQ_X, EQ_Y, x3, y3, c3)
    gamma_part = product(from_ext(e0), from_field(z0))
    dots_a[dev] = pack_dots([gamma_part, delta_part])
    spread_row(dots_a, 2, True)
    arrive(round_3)
    extend_into(e1, u1, x3, y3, c3)

    start_coarse(e1, coarse_b, 1)
    local_solve(e1, s1)
    add_coarse(s1, finish_coarse(coarse_b, 1))
    round_4 = exchange(3, s1, QF_X, QF_Y, x4, y4, c4)
    bulk_wait(dots_a, bulk_recv.at[2], n_dev)
    dots_b[grp] = add_slots(dots_a, n_dev)
    spread_row(dots_b, 3, False)
    bulk_wait(dots_b, bulk_recv.at[3], n_grp)
    first_dots = add_slots(dots_b, n_grp)
    gamma_0 = unpack_dot(first_dots, 0)
    delta_0 = unpack_dot(first_dots, 1)
    alpha_0 = gamma_0 / delta_0
    arrive(round_4)
    for i in range(NP):
        z1[i] = z0[i] - alpha_0 * fold_field(s1, i, x4, y4, c4)

    zeta_part = operate(z1, u2)
    assemble_z(u2)
    round_5 = exchange(4, u2, Q_X, Q_Y, x5, y5, c5)
    for i in range(NP):
        res_ref[i] = e0[i + 1, 8:72, :] - alpha_0 * e1[i + 1, 8:72, :]
    gamma_part = product(from_field(res_ref), from_field(z1))
    eta_part = product(from_ext(e1), from_field(z1))
    dots_c[dev] = pack_dots([gamma_part, eta_part, zeta_part])
    spread_row(dots_c, 4, True)
    bulk_wait(dots_c, bulk_recv.at[4], n_dev)
    dots_d[grp] = add_slots(dots_c, n_dev)
    spread_row(dots_d, 5, False)
    arrive(round_5)
    for i in range(NP):
        row = u2[i]
        low = y5[0, i]
        high = y5[1, i]
        if i == 0:
            row = row + x5[0, 0]
            low = low + c5[0, 0, 0]
            high = high + c5[0, 1, 0]
        elif i == NP - 1:
            row = row + x5[1, 0]
            low = low + c5[1, 0, 0]
            high = high + c5[1, 1, 0]
        e0[i, 0:8, :] = row[0:8] + low * low_wall
        e0[i, 8:56, :] = row[8:56]
        e0[i, 56:64, :] = row[56:64] + high * high_wall
    bulk_wait(dots_d, bulk_recv.at[5], n_grp)
    last_dots = add_slots(dots_d, n_grp)
    gamma_1 = unpack_dot(last_dots, 0)
    eta = unpack_dot(last_dots, 1)
    zeta = unpack_dot(last_dots, 2)
    beta = gamma_1 / gamma_0
    alpha_1 = gamma_1 / (zeta + beta * (2.0 * eta + beta * delta_0))
    scale_0 = alpha_0 + alpha_1 * beta
    for i in range(NP):
        sol_ref[i] = scale_0 * z0[i] + alpha_1 * z1[i]
        res_ref[i] = res_ref[i] - alpha_1 * (e0[i, 0:64, :] + beta * e1[i + 1, 8:72, :])

    for copies in (round_1, round_2, round_3, round_4, round_5):
        for copy in copies:
            copy.wait_send()
    for number, (buf, count) in enumerate(
        (
            (coarse_a, n_dev),
            (coarse_b, n_dev),
            (dots_a, n_dev),
            (dots_b, n_grp),
            (dots_c, n_dev),
            (dots_d, n_grp),
        )
    ):
        bulk_wait(buf, bulk_send.at[number], count)


def local(n_grp, n_dev, forcing, coefficient, coarse_inverse):
    tabs = constants()
    field = (NP, NP * NP, LANES)
    vmem = pl.BlockSpec(memory_space=pltpu.VMEM)

    def buffers(depth):
        return [
            pltpu.VMEM((2, depth, NP * NP, LANES), jnp.float32),
            pltpu.VMEM((2, NP, NP * depth, LANES), jnp.float32),
            pltpu.VMEM((2, 2, depth, NP * depth, LANES), jnp.float32),
        ]

    ext = pltpu.VMEM((NX, 128, LANES), jnp.float32)
    full = pltpu.VMEM(field, jnp.float32)
    modes = pltpu.VMEM((NX, KROWS, LANES), jnp.float32)
    along_dev = pltpu.VMEM((n_dev, 1, LANES), jnp.float32)
    along_grp = pltpu.VMEM((n_grp, 1, LANES), jnp.float32)
    out = jax.ShapeDtypeStruct(field, jnp.float32)
    columns = n_dev * coarse_inverse.shape[0]
    solved, residual = pl.pallas_call(
        functools.partial(kernel, n_grp, n_dev),
        out_shape=(out, out),
        in_specs=[vmem] * 7,
        out_specs=(vmem, vmem),
        scratch_shapes=[
            full, full, full, ext, ext, ext, ext, full, full, modes, modes,
            *buffers(2), *buffers(2), *buffers(2), *buffers(2), *buffers(1),
            along_dev, along_dev, along_dev, along_grp, along_dev, along_grp,
            pltpu.SemaphoreType.DMA((5, 8)),
            pltpu.SemaphoreType.DMA((5, 8)),
            pltpu.SemaphoreType.DMA((6,)),
            pltpu.SemaphoreType.DMA((6,)),
        ],
        compiler_params=pltpu.CompilerParams(
            collective_id=0, has_side_effects=True, vmem_limit_bytes=40 * 1024 * 1024
        ),
    )(
        forcing.reshape(field),
        coefficient.reshape(1, LANES),
        coarse_inverse[:, :columns],
        jnp.asarray(tabs["table"]),
        jnp.asarray(tabs["forward"]),
        jnp.asarray(tabs["back"]),
        jnp.asarray(tabs["plane"]),
    )
    return solved.reshape(forcing.shape), residual.reshape(forcing.shape)


def solution(mesh):
    in_specs = (
        P(None, None, None, "dev", "grp", None),
        P("dev", "grp", None),
        P(("grp", "dev"), None),
    )
    out_specs = (P(None, None, None, "dev", "grp", None), P(None, None, None, "dev", "grp", None))
    return jax.shard_map(
        functools.partial(local, mesh.shape["grp"], mesh.shape["dev"]),
        mesh=mesh,
        in_specs=in_specs,
        out_specs=out_specs,
        check_vma=False,
    )
```

```python
import functools
import math

import jax
import jax.numpy as jnp
import ml_dtypes
import numpy as np
from jax import lax
from jax.experimental import pallas as pl
from jax.experimental.pallas import tpu as pltpu
from jax.sharding import PartitionSpec as P

NP = 8
NX = NP + 2
LANES = 128
MASS_SHIFT = 0.1
HIGHEST = lax.Precision.HIGHEST


def legendre_pair(order, point):
    before = 1.0
    current = point
    for degree in range(2, order + 1):
        before, current = (
            current,
            ((2 * degree - 1) * point * current - (degree - 1) * before) / degree,
        )
    return (before, current)


def jacobi_eigen(matrix_in):
    count = len(matrix_in)
    work = [list(row_vals) for row_vals in matrix_in]
    vectors = [
        [1.0 if row_id == col_id else 0.0 for col_id in range(count)] for row_id in range(count)
    ]
    for sweep_id in range(14):
        for first_id in range(count - 1):
            for second_id in range(first_id + 1, count):
                off_value = work[first_id][second_id]
                if abs(off_value) > 1e-300:
                    theta = (work[second_id][second_id] - work[first_id][first_id]) / (
                        2.0 * off_value
                    )
                    sign_val = 1.0 if theta >= 0.0 else -1.0
                    tangent = sign_val / (abs(theta) + math.sqrt(theta * theta + 1.0))
                    cosine = 1.0 / math.sqrt(tangent * tangent + 1.0)
                    sine = tangent * cosine
                    for other_id in range(count):
                        left_val = work[other_id][first_id]
                        right_val = work[other_id][second_id]
                        work[other_id][first_id] = cosine * left_val - sine * right_val
                        work[other_id][second_id] = sine * left_val + cosine * right_val
                    for other_id in range(count):
                        left_val = work[first_id][other_id]
                        right_val = work[second_id][other_id]
                        work[first_id][other_id] = cosine * left_val - sine * right_val
                        work[second_id][other_id] = sine * left_val + cosine * right_val
                    for other_id in range(count):
                        left_val = vectors[other_id][first_id]
                        right_val = vectors[other_id][second_id]
                        vectors[other_id][first_id] = cosine * left_val - sine * right_val
                        vectors[other_id][second_id] = sine * left_val + cosine * right_val
    return ([work[idx_val][idx_val] for idx_val in range(count)], vectors)


def element_tables(point_count):
    poly_order = point_count - 1
    points = [-math.cos(math.pi * idx_val / poly_order) for idx_val in range(point_count)]
    for newton_id in range(100):
        updated = []
        for point in points:
            before, current = legendre_pair(poly_order, point)
            updated.append(point - (point * current - before) / (point_count * current))
        points = updated
    values = [legendre_pair(poly_order, point)[1] for point in points]
    weights = [2.0 / (poly_order * point_count * value**2) for value in values]
    derivative = [[0.0] * point_count for row_id in range(point_count)]
    for left_index in range(point_count):
        for right_index in range(point_count):
            if left_index != right_index:
                derivative[left_index][right_index] = values[left_index] / (
                    values[right_index] * (points[left_index] - points[right_index])
                )
    derivative[0][0] = -poly_order * point_count / 4.0
    derivative[poly_order][poly_order] = poly_order * point_count / 4.0
    stiffness = [
        [
            sum(
                (
                    derivative[inner_id][row_id] * weights[inner_id] * derivative[inner_id][col_id]
                    for inner_id in range(point_count)
                )
            )
            for col_id in range(point_count)
        ]
        for row_id in range(point_count)
    ]
    size_three = 3 * poly_order + 1
    stiff_three = [[0.0] * size_three for row_id in range(size_three)]
    mass_three = [0.0] * size_three
    for element in range(3):
        first_node = element * poly_order
        for row_id in range(point_count):
            mass_three[first_node + row_id] += weights[row_id]
            for col_id in range(point_count):
                stiff_three[first_node + row_id][first_node + col_id] += stiffness[row_id][col_id]
    keep = list(range(poly_order - 1, 2 * poly_order + 2))
    scale_half = [1.0 / math.sqrt(mass_three[idx_val]) for idx_val in keep]
    scaled = [
        [
            scale_half[row_id] * stiff_three[keep[row_id]][keep[col_id]] * scale_half[col_id]
            for col_id in range(len(keep))
        ]
        for row_id in range(len(keep))
    ]
    eigen_values, vectors = jacobi_eigen(scaled)
    transform = [
        [scale_half[row_id] * vectors[row_id][col_id] for col_id in range(len(keep))]
        for row_id in range(len(keep))
    ]
    return (weights, stiffness, eigen_values, transform)


KROWS = 112
OUTER = ((0, 1), (8, 9))
INNER = ((2, 3), (4, 5), (6, 7))
CORNERS = ((1, 1), (1, -1), (-1, 1), (-1, -1))
ALONG_X = ((1, 0), (-1, 0))
ALONG_Y = ((0, 1), (0, -1))
SIDES = CORNERS + ALONG_X + ALONG_Y
FORWARD = 128
BACK = FORWARD + 2 * KROWS
PLANE = BACK + 2 * KROWS
TABLE_ROWS = PLANE + 2 * 64


def split_bf16(matrix):
    high = matrix.astype(ml_dtypes.bfloat16)
    low = (matrix - high.astype(np.float64)).astype(ml_dtypes.bfloat16)
    return high, low


def padded_parts(matrix):
    parts = np.zeros((2 * matrix.shape[0], LANES), np.float32)
    for index, part in enumerate(split_bf16(matrix)):
        rows = slice(index * matrix.shape[0], (index + 1) * matrix.shape[0])
        parts[rows, : matrix.shape[1]] = part.astype(np.float32)
    return parts


@functools.lru_cache(maxsize=None)
def constants():
    weights, stiffness, eigen_values, transform = (
        np.array(table, dtype=np.float64) for table in element_tables(NP)
    )
    forward = np.zeros((KROWS, KROWS))
    lam_rows = np.zeros((KROWS,))
    for b in range(NX):
        for c in range(NX):
            row = b * NX + c
            lam_rows[row] = eigen_values[b] + eigen_values[c]
            for j in range(NX):
                for k in range(NX):
                    if k == 0:
                        col = 80 + j
                    elif k == NX - 1:
                        col = 96 + j
                    else:
                        col = j * NP + k - 1
                    forward[row, col] = transform[j, b] * transform[k, c]
    diag_w = np.diag(weights)
    plane = np.kron(stiffness, diag_w) + np.kron(diag_w, stiffness)
    table = np.zeros((128, LANES), np.float32)
    table[:KROWS] = lam_rows[:, None]
    table[KROWS : KROWS + NP] = weights[:, None]
    half = np.ones((NP,))
    half[0] = half[-1] = 0.5
    table[KROWS + NP :] = half[:, None]
    return dict(
        weights=[float(v) for v in weights],
        stiffness=stiffness,
        eigen=[float(v) for v in eigen_values],
        transform=transform,
        table=np.concatenate(
            [table, padded_parts(forward), padded_parts(forward.T), padded_parts(plane)], 0
        ),
    )


def combine(scalars, vectors):
    total = None
    for scalar, vector in zip(scalars, vectors):
        term = float(scalar) * vector
        total = term if total is None else total + term
    return total


def dot_split(matrix, value):
    rows = value.shape[0]
    high = value.astype(jnp.bfloat16)
    low = (value - high.astype(jnp.float32)).astype(jnp.bfloat16)
    parts = [high, low]
    gap = matrix.shape[1] // 2 - rows
    if gap > 0:
        zeros = jnp.zeros((gap, value.shape[1]), jnp.bfloat16)
        parts = [high, zeros, low, zeros]
    out = jnp.dot(
        matrix, jnp.concatenate(parts, axis=0), preferred_element_type=jnp.float32
    )
    return out[:rows] + out[rows:]


def lane_fold(value):
    value = value + pltpu.roll(value, 64, 1)
    return value + pltpu.roll(value, 32, 1)


def next_lane(value, axis):
    return pltpu.roll(value, LANES - 1, axis)


def previous_lane(value, axis):
    return pltpu.roll(value, 1, axis)


def face_range(step, low, middle, high):
    return {1: high, -1: low, 0: middle}[step]


EQ_X = (slice(0, 2), slice(0, 8), slice(6, 8))
EQ_Y = (slice(0, 16), slice(0, 64), slice(48, 64))
QF_X = (slice(0, 2), slice(1, 9), slice(8, 10))
QF_Y = (slice(0, 16), slice(8, 72), slice(64, 80))
Q_X = (slice(0, 1), slice(0, 8), slice(7, 8))
Q_Y = (slice(0, 8), slice(0, 64), slice(56, 64))


def kernel(
    n_grp,
    n_dev,
    f_hbm,
    coef_hbm,
    rows_hbm,
    table_hbm,
    sol_ref,
    res_ref,
    coef_ref,
    rows_ref,
    table_ref,
    fwd_ref,
    back_ref,
    plane_ref,
    pick_ref,
    u0,
    u1,
    u2,
    e0,
    e1,
    s0,
    s1,
    z0,
    z1,
    work,
    inv_ref,
    x1,
    y1,
    c1,
    x2,
    y2,
    c2,
    x3,
    y3,
    c3,
    x4,
    y4,
    c4,
    x5,
    y5,
    c5,
    part_a,
    part_b,
    sums_a,
    sums_b,
    dots_a,
    dots_b,
    dots_c,
    dots_d,
    load_sem,
    send_sem,
    recv_sem,
    bulk_send,
    bulk_recv,
):
    tabs = constants()
    weights = tabs["weights"]
    stiff = tabs["stiffness"]
    trans = tabs["transform"]
    eigen = tabs["eigen"]
    grp = lax.axis_index("grp")
    dev = lax.axis_index("dev")

    def dev_at(step):
        return lax.rem(dev + step + n_dev, n_dev)

    def grp_at(step):
        return lax.rem(grp + step + n_grp, n_grp)

    loads = [
        pltpu.make_async_copy(src, dst, load_sem.at[index])
        for index, (src, dst) in enumerate(
            (
                (f_hbm, u0),
                (table_hbm, table_ref),
                (coef_hbm, coef_ref),
                (rows_hbm, rows_ref),
            )
        )
    ]
    for load in loads:
        load.start()

    barrier = pltpu.get_barrier_semaphore()

    def greet_dev(step, carry):
        pl.semaphore_signal(
            barrier, inc=1, device_id=(grp, lax.rem(dev + step, n_dev)),
            device_id_type=pl.DeviceIdType.MESH,
        )
        return carry

    def greet_grp(step, carry):
        pl.semaphore_signal(
            barrier, inc=1, device_id=(lax.rem(grp + step, n_grp), dev),
            device_id_type=pl.DeviceIdType.MESH,
        )
        return carry

    lax.fori_loop(1, n_dev, greet_dev, 0)
    lax.fori_loop(1, n_grp, greet_grp, 0)
    for dx, dy in CORNERS:
        pl.semaphore_signal(
            barrier, inc=1, device_id=(grp_at(dy), dev_at(dx)),
            device_id_type=pl.DeviceIdType.MESH,
        )

    def exchange(number, sides, source, x_ranges, y_ranges, x_buf, y_buf, c_buf):
        copies = []
        for dx, dy in sides:
            index = SIDES.index((dx, dy))
            src = source.at[
                face_range(dx, *x_ranges), face_range(dy, *y_ranges), :
            ]
            if dy == 0:
                dst = x_buf.at[0 if dx == 1 else 1]
            elif dx == 0:
                dst = y_buf.at[0 if dy == 1 else 1]
            else:
                dst = c_buf.at[0 if dx == 1 else 1, 0 if dy == 1 else 1]
            copy = pltpu.make_async_remote_copy(
                src_ref=src,
                dst_ref=dst,
                send_sem=send_sem.at[number, index],
                recv_sem=recv_sem.at[number, index],
                device_id=(grp_at(dy), dev_at(dx)),
                device_id_type=pl.DeviceIdType.MESH,
            )
            copy.start()
            copies.append(copy)
        return copies

    def arrive(copies):
        for copy in copies:
            copy.wait_recv()

    def send_row(src, dst, number, where):
        pltpu.make_async_remote_copy(
            src_ref=src,
            dst_ref=dst,
            send_sem=bulk_send.at[number],
            recv_sem=bulk_recv.at[number],
            device_id=where,
            device_id_type=pl.DeviceIdType.MESH,
        ).start()

    def spread_row(buf, number, along_dev):
        count = n_dev if along_dev else n_grp
        me = dev if along_dev else grp

        def body(step, carry):
            other = lax.rem(me + step, count)
            send_row(buf.at[me], buf.at[me], number, (grp, other) if along_dev else (other, dev))
            return carry

        lax.fori_loop(1, count, body, 0)

    def bulk_wait(buf, sem, count):
        part = buf.at[pl.ds(0, count)]
        pltpu.make_async_copy(part, part, sem).wait()

    low_wall = jnp.where(grp == 0, 0.0, 1.0).astype(jnp.float32)
    high_wall = jnp.where(grp == n_grp - 1, 0.0, 1.0).astype(jnp.float32)
    lane = lax.broadcasted_iota(jnp.int32, (1, LANES), 1)

    def assemble_z(ref):
        top = ref[:, pl.ds(0, NP, stride=NP), :]
        bottom = ref[:, pl.ds(NP - 1, NP, stride=NP), :]
        ref[:, pl.ds(0, NP, stride=NP), :] = top + previous_lane(bottom, 2)
        ref[:, pl.ds(NP - 1, NP, stride=NP), :] = bottom + next_lane(top, 2)

    loads[0].wait()
    assemble_z(u0)
    pl.semaphore_wait(barrier, n_dev - 1 + n_grp - 1 + 4)
    round_1 = exchange(0, SIDES, u0, EQ_X, EQ_Y, x1, y1, c1)
    for load in loads[1:]:
        load.wait()

    coef = coef_ref[...]
    w_k = table_ref[KROWS : KROWS + NP, :]
    half_k = table_ref[KROWS + NP : FORWARD, :]
    for ref, first in ((fwd_ref, FORWARD), (back_ref, BACK)):
        high = table_ref[first : first + KROWS, :].astype(jnp.bfloat16)
        low = table_ref[first + KROWS : first + 2 * KROWS, :].astype(jnp.bfloat16)
        ref[0:KROWS, 0:LANES] = high
        ref[0:KROWS, LANES:] = high
        ref[KROWS:, 0:LANES] = low
        ref[KROWS:, LANES:] = jnp.zeros_like(low)
    high = table_ref[PLANE : PLANE + 64, :]
    plane_ref[0:64, :] = (high + pltpu.roll(high, 64, 1)).astype(jnp.bfloat16)
    plane_ref[64:, :] = table_ref[PLANE + 64 : PLANE + 128, :].astype(jnp.bfloat16)
    place = lax.broadcasted_iota(jnp.int32, (LANES, LANES), 0)
    elem = lax.broadcasted_iota(jnp.int32, (LANES, LANES), 1)
    for index in range(3):
        block = lax.rem(dev + index + 3, 4)
        pick_ref[:, index * LANES : (index + 1) * LANES] = jnp.where(
            place == block * 32 + lax.shift_right_logical(elem, 2), 1.0, 0.0
        ).astype(jnp.float32)
    lam_rows = table_ref[0:KROWS, :]
    for a in range(NX):
        inv_ref[a] = 1.0 / (coef * (lam_rows + eigen[a]) + MASS_SHIFT)
    zero_rows = jnp.zeros((128 - 80, LANES), jnp.float32)
    for i in range(NX):
        e0[i, 80:128, :] = zero_rows
        e1[i, 80:128, :] = zero_rows
        s0[i, 80:128, :] = zero_rows
        s1[i, 80:128, :] = zero_rows

    def extend_into(ext, layers, own, x_buf, y_buf, c_buf):
        for i in layers:
            if i == 0:
                row = x_buf[0, 0]
                low = c_buf[0, 0, 0]
                high = c_buf[0, 1, 0]
            elif i == NX - 1:
                row = x_buf[1, 1]
                low = c_buf[1, 0, 1]
                high = c_buf[1, 1, 1]
            else:
                row = own[i - 1]
                low = y_buf[0, i - 1]
                high = y_buf[1, i - 1]
                if i == 1:
                    row = row + x_buf[0, 1]
                    low = low + c_buf[0, 0, 1]
                    high = high + c_buf[0, 1, 1]
                elif i == NX - 2:
                    row = row + x_buf[1, 0]
                    low = low + c_buf[1, 0, 0]
                    high = high + c_buf[1, 1, 0]
            low = low * low_wall
            high = high * high_wall
            ext[i, 0:8, :] = low[0:8]
            ext[i, 8:16, :] = row[0:8] + low[8:16]
            ext[i, 16:64, :] = row[8:56]
            ext[i, 64:72, :] = row[56:64] + high[0:8]
            ext[i, 72:80, :] = high[8:16]

    def start_coarse(ext, part, sums, number):
        total = None
        for i in range(NP):
            line = combine(
                weights, [ext[i + 1, 8 + NP * j : 16 + NP * j, :] for j in range(NP)]
            )
            total = weights[i] * line if total is None else total + weights[i] * line
        total = jnp.sum(total * w_k, axis=0, keepdims=True)
        unknown = lax.broadcasted_iota(jnp.int32, (32, LANES), 0)
        elem = lax.broadcasted_iota(jnp.int32, (32, LANES), 1)
        mine = lax.shift_right_logical(elem, 2) == unknown
        column = jnp.sum(jnp.where(mine, total, 0.0), axis=1, keepdims=True)
        count = n_dev // 4
        pieces = [
            jnp.sum(rows_ref[:, m * LANES : (m + 1) * LANES] * column, axis=0, keepdims=True)
            for m in range(count)
        ]
        for m in range(count):
            first = jnp.where(lane >= 96, pieces[(m - 1) % count], pieces[m])
            last = jnp.where(lane < 32, pieces[(m + 1) % count], pieces[m])
            for index, row in enumerate((first, pieces[m], pieces[m], last)):
                part[4 * m + index] = row
        sums[1, dev] = part[dev]
        up = grp_at(1)
        down = grp_at(-1)

        def send(step, carry):
            other = lax.rem(dev + step, n_dev)
            send_row(part.at[other], sums.at[0, dev], number, (up, other))
            send_row(part.at[other], sums.at[2, dev], number + 2, (down, other))
            return carry

        def send_own(step, carry):
            other = lax.rem(dev + step, n_dev)
            send_row(part.at[other], sums.at[1, dev], number + 1, (grp, other))
            return send(step, carry)

        lax.fori_loop(1, n_dev, send_own, 0)
        send(0, 0)

    def coarse_wait(sums, sem, number):
        bulk_wait(sums.at[0], sem.at[number], n_dev)
        bulk_wait(sums.at[1], sem.at[number + 1], n_dev - 1)
        bulk_wait(sums.at[2], sem.at[number + 2], n_dev)

    def finish_coarse(sums, number):
        coarse_wait(sums, bulk_recv, number)
        totals = [add_slots(sums.at[index], n_dev) for index in range(3)]
        totals = jnp.concatenate(
            [totals[0] * low_wall, totals[1], totals[2] * high_wall]
            + [jnp.zeros((5, LANES), jnp.float32)],
            axis=0,
        )
        spread = jnp.dot(
            totals, pick_ref[...], precision=HIGHEST, preferred_element_type=jnp.float32
        )
        before, here, after = (spread[:, m * LANES : (m + 1) * LANES] for m in range(3))
        node = lax.broadcasted_iota(jnp.int32, (NP, LANES), 0)
        out = []
        for value in (here + before, here, here + after):
            left = previous_lane(value, 1)
            right = next_lane(value, 1)
            lines = []
            for index in range(3):
                row = slice(index, index + 1)
                lines.append(
                    w_k
                    * (
                        value[row]
                        + jnp.where(node == 0, left[row], 0.0)
                        + jnp.where(node == NP - 1, right[row], 0.0)
                    )
                )
            out.append((lines[1] + lines[0], lines[1], lines[1] + lines[2]))
        return out

    even = [a for a in range(NX) if abs(trans[0, a] - trans[9, a]) < abs(trans[0, a] + trans[9, a])]
    odd = [a for a in range(NX) if a not in even]

    def forward(ext, pairs):
        for pair in pairs:
            parts = []
            for i in pair:
                front = previous_lane(ext[i, pl.ds(6, 16, stride=NP), :], 1)
                behind = next_lane(ext[i, pl.ds(1, 16, stride=NP), :], 1)
                parts.append(jnp.concatenate([ext[i, 0:80, :], front, behind], axis=0))
            got = dot_split(fwd_ref[...], jnp.concatenate(parts, axis=1))
            work[pair[0]] = got[:, 0:LANES]
            work[pair[1]] = got[:, LANES:]

    def solve_modes():
        def middle(block, carry):
            rows = pl.ds(pl.multiple_of(block * 8, 8), 8)
            vals = [work[i, rows, :] for i in range(NX)]
            plus = [vals[i] + vals[NX - 1 - i] for i in range(5)]
            minus = [vals[i] - vals[NX - 1 - i] for i in range(5)]
            modes = {}
            for a in range(NX):
                source = plus if a in even else minus
                modes[a] = combine(trans[:5, a], source) * inv_ref[a, rows, :]
            for i in range(5):
                sym = combine(trans[i, even], [modes[a] for a in even])
                anti = combine(trans[i, odd], [modes[a] for a in odd])
                work[i, rows, :] = sym + anti
                work[NX - 1 - i, rows, :] = sym - anti
            return carry

        lax.fori_loop(0, KROWS // 8 - 1, middle, 0)

    def backward(out, pairs):
        for pair in pairs:
            got = dot_split(
                back_ref[...], jnp.concatenate([work[pair[0]], work[pair[1]]], axis=1)
            )
            for side, i in enumerate(pair):
                part = got[:, side * LANES : (side + 1) * LANES]
                out[i, 0:80, :] = part[0:80]
                at_6 = pl.ds(6, 16, stride=NP)
                at_1 = pl.ds(1, 16, stride=NP)
                at_0 = pl.ds(0, 16, stride=NP)
                at_7 = pl.ds(7, 16, stride=NP)
                out[i, at_6, :] = out[i, at_6, :] + next_lane(part[80:96], 1)
                out[i, at_1, :] = out[i, at_1, :] + previous_lane(part[96:112], 1)
                top = out[i, at_0, :]
                bottom = out[i, at_7, :]
                out[i, at_0, :] = top + previous_lane(bottom, 1)
                out[i, at_7, :] = bottom + next_lane(top, 1)

    def extend_and_solve(arriving, ext, own, buffers, part, sums, number, out, between):
        arrive(arriving[6:8])
        extend_into(ext, range(2, 8), own, *buffers)
        forward(ext, INNER)
        arrive(arriving[4:6])
        arrive(arriving[0:4])
        extend_into(ext, (0, 1, 8, 9), own, *buffers)
        start_coarse(ext, part, sums, number)
        forward(ext, OUTER)
        between()
        solve_modes()
        backward(out, OUTER)

    def send_folds(number, out, buffers):
        copies = exchange(number, CORNERS + ALONG_X, out, QF_X, QF_Y, *buffers)
        backward(out, INNER)
        return copies + exchange(number, ALONG_Y, out, QF_X, QF_Y, *buffers)

    def fold_field(out, coarse, i, x_buf, y_buf, c_buf):
        row = out[i + 1, 8:72, :]
        low = y_buf[0, i]
        high = y_buf[1, i]
        if i < 2:
            row = row + x_buf[0, i]
            low = low + c_buf[0, 0, i]
            high = high + c_buf[0, 1, i]
        elif i >= 6:
            row = row + x_buf[1, i - 6]
            low = low + c_buf[1, 0, i - 6]
            high = high + c_buf[1, 1, i - 6]
        lines = coarse[0 if i == 0 else 2 if i == NP - 1 else 1]
        terms = [
            (weights[i] * weights[j]) * lines[0 if j == 0 else 2 if j == NP - 1 else 1]
            for j in range(NP)
        ]
        return jnp.concatenate(
            [row[0:16] + low * low_wall, row[16:48], row[48:64] + high * high_wall], axis=0
        ) + jnp.concatenate(terms, axis=0)

    def operate(field, out):
        total = jnp.zeros((NP, LANES), jnp.float32)
        for pair in ((0, 7), (1, 6), (2, 5), (3, 4)):
            got = dot_split(
                plane_ref[...], jnp.concatenate([field[pair[0]], field[pair[1]]], axis=1)
            )
            out[pair[0]] = got[:, 0:LANES]
            out[pair[1]] = got[:, LANES:]
        for j in range(NP):
            rows = slice(NP * j, NP * j + NP)
            vals = [field[i, rows, :] for i in range(NP)]
            plus = [vals[i] + vals[NP - 1 - i] for i in range(4)]
            minus = [vals[i] - vals[NP - 1 - i] for i in range(4)]
            w_yz = weights[j] * w_k
            coef_yz = coef * w_yz
            for i in range(4):
                sym = combine([(stiff[i, m] + stiff[i, 7 - m]) / 2 for m in range(4)], plus)
                anti = combine([(stiff[i, m] - stiff[i, 7 - m]) / 2 for m in range(4)], minus)
                for at, value in ((i, sym + anti), (7 - i, sym - anti)):
                    result = (
                        value * coef_yz
                        + (weights[at] * coef) * out[at, rows, :]
                        + (MASS_SHIFT * weights[at]) * (w_yz * vals[at])
                    )
                    out[at, rows, :] = result
                    total = total + result * vals[at]
        return total

    def product(left, right):
        total = jnp.zeros((NP, LANES), jnp.float32)
        for j in range(NP):
            line = None
            for i in range(NP):
                term = left(i, j) * right(i, j)
                if i in (0, NP - 1):
                    term = 0.5 * term
                line = term if line is None else line + term
            if j == 0:
                line = line * (1.0 - 0.5 * low_wall)
            elif j == NP - 1:
                line = line * (1.0 - 0.5 * high_wall)
            total = total + line
        return total * half_k

    def from_ext(ext):
        return lambda i, j: ext[i + 1, 8 + NP * j : 16 + NP * j, :]

    def from_field(field):
        return lambda i, j: field[i, NP * j : NP * j + NP, :]

    def pack_dots(totals):
        packed = None
        for index, total in enumerate(totals):
            row = lane_fold(jnp.sum(total, axis=0, keepdims=True))
            mine = (lane >= 32 * index) & (lane < 32 * index + 32)
            row = jnp.where(mine, row, 0.0)
            packed = row if packed is None else packed + row
        return packed

    def unpack_dot(row, index):
        mine = (lane >= 32 * index) & (lane < 32 * index + 32)
        return jnp.sum(jnp.where(mine, row, 0.0), axis=1, keepdims=True)

    def add_slots(buf, count):
        rows = [buf[index] for index in range(count)]
        while len(rows) > 1:
            rows = [rows[index] + rows[index + 1] for index in range(0, len(rows), 2)]
        return rows[0]

    extend_and_solve(
        round_1, e0, u0, (x1, y1, c1), part_a, sums_a, 0, s0, lambda: None
    )
    round_2 = send_folds(1, s0, (x2, y2, c2))
    arrive(round_2)
    coarse = finish_coarse(sums_a, 0)
    for i in range(NP):
        z0[i] = fold_field(s0, coarse, i, x2, y2, c2)

    delta_part = operate(z0, u1)
    assemble_z(u1)
    round_3 = exchange(2, SIDES, u1, EQ_X, EQ_Y, x3, y3, c3)
    gamma_part = product(from_ext(e0), from_field(z0))
    dots_a[dev] = pack_dots([gamma_part, delta_part])
    spread_row(dots_a, 6, True)

    def second_half():
        bulk_wait(dots_a, bulk_recv.at[6], n_dev - 1)
        dots_b[grp] = add_slots(dots_a, n_dev)
        spread_row(dots_b, 7, False)

    extend_and_solve(
        round_3, e1, u1, (x3, y3, c3), part_b, sums_b, 3, s1, second_half
    )
    round_4 = send_folds(3, s1, (x4, y4, c4))
    bulk_wait(dots_b, bulk_recv.at[7], n_grp - 1)
    first_dots = add_slots(dots_b, n_grp)
    gamma_0 = unpack_dot(first_dots, 0)
    delta_0 = unpack_dot(first_dots, 1)
    alpha_0 = gamma_0 / delta_0
    for i in range(NP):
        res_ref[i] = e0[i + 1, 8:72, :] - alpha_0 * e1[i + 1, 8:72, :]
    arrive(round_4)
    coarse = finish_coarse(sums_b, 3)
    for i in range(NP):
        z1[i] = z0[i] - alpha_0 * fold_field(s1, coarse, i, x4, y4, c4)

    gamma_part = product(from_field(res_ref), from_field(z1))
    eta_part = product(from_ext(e1), from_field(z1))
    zeta_part = operate(z1, u2)
    dots_c[dev] = pack_dots([gamma_part, eta_part, zeta_part])
    spread_row(dots_c, 8, True)
    assemble_z(u2)
    round_5 = exchange(4, SIDES, u2, Q_X, Q_Y, x5, y5, c5)
    bulk_wait(dots_c, bulk_recv.at[8], n_dev - 1)
    dots_d[grp] = add_slots(dots_c, n_dev)
    spread_row(dots_d, 9, False)
    arrive(round_5)
    for i in range(NP):
        row = u2[i]
        low = y5[0, i]
        high = y5[1, i]
        if i == 0:
            row = row + x5[0, 0]
            low = low + c5[0, 0, 0]
            high = high + c5[0, 1, 0]
        elif i == NP - 1:
            row = row + x5[1, 0]
            low = low + c5[1, 0, 0]
            high = high + c5[1, 1, 0]
        e0[i, 0:8, :] = row[0:8] + low * low_wall
        e0[i, 8:56, :] = row[8:56]
        e0[i, 56:64, :] = row[56:64] + high * high_wall
    bulk_wait(dots_d, bulk_recv.at[9], n_grp - 1)
    last_dots = add_slots(dots_d, n_grp)
    gamma_1 = unpack_dot(last_dots, 0)
    eta = unpack_dot(last_dots, 1)
    zeta = unpack_dot(last_dots, 2)
    beta = gamma_1 / gamma_0
    alpha_1 = gamma_1 / (zeta + beta * (2.0 * eta + beta * delta_0))
    scale_0 = alpha_0 + alpha_1 * beta
    for i in range(NP):
        sol_ref[i] = scale_0 * z0[i] + alpha_1 * z1[i]
        res_ref[i] = res_ref[i] - alpha_1 * (e0[i, 0:64, :] + beta * e1[i + 1, 8:72, :])

    for copies in (round_1, round_2, round_3, round_4, round_5):
        for copy in copies:
            copy.wait_send()
    coarse_wait(sums_a, bulk_send, 0)
    coarse_wait(sums_b, bulk_send, 3)
    for number, buf, count in (
        (6, dots_a, n_dev),
        (7, dots_b, n_grp),
        (8, dots_c, n_dev),
        (9, dots_d, n_grp),
    ):
        bulk_wait(buf, bulk_send.at[number], count - 1)


def local(n_grp, n_dev, forcing, coefficient, coarse_inverse):
    tabs = constants()
    field = (NP, NP * NP, LANES)
    vmem = pl.BlockSpec(memory_space=pltpu.VMEM)

    def buffers(depth):
        return [
            pltpu.VMEM((2, depth, NP * NP, LANES), jnp.float32),
            pltpu.VMEM((2, NP, NP * depth, LANES), jnp.float32),
            pltpu.VMEM((2, 2, depth, NP * depth, LANES), jnp.float32),
        ]

    ext = pltpu.VMEM((NX, 128, LANES), jnp.float32)
    full = pltpu.VMEM(field, jnp.float32)
    modes = pltpu.VMEM((NX, KROWS, LANES), jnp.float32)
    along_dev = pltpu.VMEM((n_dev, 1, LANES), jnp.float32)
    along_grp = pltpu.VMEM((n_grp, 1, LANES), jnp.float32)
    three_groups = pltpu.VMEM((3, n_dev, 1, LANES), jnp.float32)
    out = jax.ShapeDtypeStruct(field, jnp.float32)
    columns = n_dev * coarse_inverse.shape[0]
    solved, residual = pl.pallas_call(
        functools.partial(kernel, n_grp, n_dev),
        out_shape=(out, out),
        in_specs=[pl.BlockSpec(memory_space=pltpu.HBM)] * 4,
        out_specs=(vmem, vmem),
        scratch_shapes=[
            pltpu.VMEM((1, LANES), jnp.float32),
            pltpu.VMEM(coarse_inverse[:, :columns].shape, jnp.float32),
            pltpu.VMEM((TABLE_ROWS, LANES), jnp.float32),
            pltpu.VMEM((2 * KROWS, 2 * LANES), jnp.bfloat16),
            pltpu.VMEM((2 * KROWS, 2 * LANES), jnp.bfloat16),
            pltpu.VMEM((128, LANES), jnp.bfloat16),
            pltpu.VMEM((LANES, 3 * LANES), jnp.float32),
            full, full, full, ext, ext, ext, ext, full, full, modes, modes,
            *buffers(2), *buffers(2), *buffers(2), *buffers(2), *buffers(1),
            along_dev, along_dev, three_groups, three_groups,
            along_dev, along_grp, along_dev, along_grp,
            pltpu.SemaphoreType.DMA((4,)),
            pltpu.SemaphoreType.DMA((5, 8)),
            pltpu.SemaphoreType.DMA((5, 8)),
            pltpu.SemaphoreType.DMA((10,)),
            pltpu.SemaphoreType.DMA((10,)),
        ],
        compiler_params=pltpu.CompilerParams(
            collective_id=0, has_side_effects=True, vmem_limit_bytes=40 * 1024 * 1024
        ),
    )(
        *(
            pltpu.with_memory_space_constraint(array, pltpu.HBM)
            for array in (
                forcing.reshape(field),
                coefficient.reshape(1, LANES),
                coarse_inverse[:, :columns],
                jnp.asarray(tabs["table"]),
            )
        )
    )
    return solved.reshape(forcing.shape), residual.reshape(forcing.shape)


def solution(mesh):
    in_specs = (
        P(None, None, None, "dev", "grp", None),
        P("dev", "grp", None),
        P(("grp", "dev"), None),
    )
    out_specs = (P(None, None, None, "dev", "grp", None), P(None, None, None, "dev", "grp", None))
    return jax.shard_map(
        functools.partial(local, mesh.shape["grp"], mesh.shape["dev"]),
        mesh=mesh,
        in_specs=in_specs,
        out_specs=out_specs,
        check_vma=False,
    )
```

```python
import functools
import math

import jax
import jax.numpy as jnp
import ml_dtypes
import numpy as np
from jax import lax
from jax.experimental import pallas as pl
from jax.experimental.pallas import tpu as pltpu
from jax.sharding import PartitionSpec as P

NP = 8
NX = NP + 2
LANES = 128
MASS_SHIFT = 0.1
HIGHEST = lax.Precision.HIGHEST


def legendre_pair(order, point):
    before = 1.0
    current = point
    for degree in range(2, order + 1):
        before, current = (
            current,
            ((2 * degree - 1) * point * current - (degree - 1) * before) / degree,
        )
    return (before, current)


def jacobi_eigen(matrix_in):
    count = len(matrix_in)
    work = [list(row_vals) for row_vals in matrix_in]
    vectors = [
        [1.0 if row_id == col_id else 0.0 for col_id in range(count)] for row_id in range(count)
    ]
    for sweep_id in range(14):
        for first_id in range(count - 1):
            for second_id in range(first_id + 1, count):
                off_value = work[first_id][second_id]
                if abs(off_value) > 1e-300:
                    theta = (work[second_id][second_id] - work[first_id][first_id]) / (
                        2.0 * off_value
                    )
                    sign_val = 1.0 if theta >= 0.0 else -1.0
                    tangent = sign_val / (abs(theta) + math.sqrt(theta * theta + 1.0))
                    cosine = 1.0 / math.sqrt(tangent * tangent + 1.0)
                    sine = tangent * cosine
                    for other_id in range(count):
                        left_val = work[other_id][first_id]
                        right_val = work[other_id][second_id]
                        work[other_id][first_id] = cosine * left_val - sine * right_val
                        work[other_id][second_id] = sine * left_val + cosine * right_val
                    for other_id in range(count):
                        left_val = work[first_id][other_id]
                        right_val = work[second_id][other_id]
                        work[first_id][other_id] = cosine * left_val - sine * right_val
                        work[second_id][other_id] = sine * left_val + cosine * right_val
                    for other_id in range(count):
                        left_val = vectors[other_id][first_id]
                        right_val = vectors[other_id][second_id]
                        vectors[other_id][first_id] = cosine * left_val - sine * right_val
                        vectors[other_id][second_id] = sine * left_val + cosine * right_val
    return ([work[idx_val][idx_val] for idx_val in range(count)], vectors)


def element_tables(point_count):
    poly_order = point_count - 1
    points = [-math.cos(math.pi * idx_val / poly_order) for idx_val in range(point_count)]
    for newton_id in range(100):
        updated = []
        for point in points:
            before, current = legendre_pair(poly_order, point)
            updated.append(point - (point * current - before) / (point_count * current))
        points = updated
    values = [legendre_pair(poly_order, point)[1] for point in points]
    weights = [2.0 / (poly_order * point_count * value**2) for value in values]
    derivative = [[0.0] * point_count for row_id in range(point_count)]
    for left_index in range(point_count):
        for right_index in range(point_count):
            if left_index != right_index:
                derivative[left_index][right_index] = values[left_index] / (
                    values[right_index] * (points[left_index] - points[right_index])
                )
    derivative[0][0] = -poly_order * point_count / 4.0
    derivative[poly_order][poly_order] = poly_order * point_count / 4.0
    stiffness = [
        [
            sum(
                (
                    derivative[inner_id][row_id] * weights[inner_id] * derivative[inner_id][col_id]
                    for inner_id in range(point_count)
                )
            )
            for col_id in range(point_count)
        ]
        for row_id in range(point_count)
    ]
    size_three = 3 * poly_order + 1
    stiff_three = [[0.0] * size_three for row_id in range(size_three)]
    mass_three = [0.0] * size_three
    for element in range(3):
        first_node = element * poly_order
        for row_id in range(point_count):
            mass_three[first_node + row_id] += weights[row_id]
            for col_id in range(point_count):
                stiff_three[first_node + row_id][first_node + col_id] += stiffness[row_id][col_id]
    keep = list(range(poly_order - 1, 2 * poly_order + 2))
    scale_half = [1.0 / math.sqrt(mass_three[idx_val]) for idx_val in keep]
    scaled = [
        [
            scale_half[row_id] * stiff_three[keep[row_id]][keep[col_id]] * scale_half[col_id]
            for col_id in range(len(keep))
        ]
        for row_id in range(len(keep))
    ]
    eigen_values, vectors = jacobi_eigen(scaled)
    transform = [
        [scale_half[row_id] * vectors[row_id][col_id] for col_id in range(len(keep))]
        for row_id in range(len(keep))
    ]
    return (weights, stiffness, eigen_values, transform)


KROWS = 112
OUTER = ((0, 1), (8, 9))
INNER = ((2, 3), (4, 5), (6, 7))
CORNERS = ((1, 1), (1, -1), (-1, 1), (-1, -1))
ALONG_X = ((1, 0), (-1, 0))
ALONG_Y = ((0, 1), (0, -1))
SIDES = CORNERS + ALONG_X + ALONG_Y
FORWARD = 128
BACK = FORWARD + 2 * KROWS
PLANE = BACK + 2 * KROWS
TABLE_ROWS = PLANE + 2 * 64


def split_bf16(matrix):
    high = matrix.astype(ml_dtypes.bfloat16)
    low = (matrix - high.astype(np.float64)).astype(ml_dtypes.bfloat16)
    return high, low


def padded_parts(matrix):
    parts = np.zeros((2 * matrix.shape[0], LANES), np.float32)
    for index, part in enumerate(split_bf16(matrix)):
        rows = slice(index * matrix.shape[0], (index + 1) * matrix.shape[0])
        parts[rows, : matrix.shape[1]] = part.astype(np.float32)
    return parts


@functools.lru_cache(maxsize=None)
def constants():
    weights, stiffness, eigen_values, transform = (
        np.array(table, dtype=np.float64) for table in element_tables(NP)
    )
    forward = np.zeros((KROWS, KROWS))
    lam_rows = np.zeros((KROWS,))
    for b in range(NX):
        for c in range(NX):
            row = b * NX + c
            lam_rows[row] = eigen_values[b] + eigen_values[c]
            for j in range(NX):
                for k in range(NX):
                    if k == 0:
                        col = 80 + j
                    elif k == NX - 1:
                        col = 96 + j
                    else:
                        col = j * NP + k - 1
                    forward[row, col] = transform[j, b] * transform[k, c]
    diag_w = np.diag(weights)
    plane = np.kron(stiffness, diag_w) + np.kron(diag_w, stiffness)
    table = np.zeros((128, LANES), np.float32)
    table[:KROWS] = lam_rows[:, None]
    table[KROWS : KROWS + NP] = weights[:, None]
    half = np.ones((NP,))
    half[0] = half[-1] = 0.5
    table[KROWS + NP :] = half[:, None]
    return dict(
        weights=[float(v) for v in weights],
        stiffness=stiffness,
        eigen=[float(v) for v in eigen_values],
        transform=transform,
        table=np.concatenate(
            [table, padded_parts(forward), padded_parts(forward.T), padded_parts(plane)], 0
        ),
    )


def combine(scalars, vectors):
    total = None
    for scalar, vector in zip(scalars, vectors):
        term = float(scalar) * vector
        total = term if total is None else total + term
    return total


def dot_split(matrix, value):
    rows = value.shape[0]
    high = value.astype(jnp.bfloat16)
    low = (value - high.astype(jnp.float32)).astype(jnp.bfloat16)
    parts = [high, low]
    gap = matrix.shape[1] // 2 - rows
    if gap > 0:
        zeros = jnp.zeros((gap, value.shape[1]), jnp.bfloat16)
        parts = [high, zeros, low, zeros]
    out = jnp.dot(
        matrix, jnp.concatenate(parts, axis=0), preferred_element_type=jnp.float32
    )
    return out[:rows] + out[rows:]


def lane_fold(value):
    value = value + pltpu.roll(value, 64, 1)
    return value + pltpu.roll(value, 32, 1)


def next_lane(value, axis):
    return pltpu.roll(value, LANES - 1, axis)


def previous_lane(value, axis):
    return pltpu.roll(value, 1, axis)


def face_range(step, low, middle, high):
    return {1: high, -1: low, 0: middle}[step]


EQ_X = (slice(0, 2), slice(0, 8), slice(6, 8))
EQ_Y = (slice(0, 16), slice(0, 64), slice(48, 64))
QF_X = (slice(0, 2), slice(1, 9), slice(8, 10))
QF_Y = (slice(0, 16), slice(8, 72), slice(64, 80))
Q_X = (slice(0, 1), slice(0, 8), slice(7, 8))
Q_Y = (slice(0, 8), slice(0, 64), slice(56, 64))


def kernel(
    n_grp,
    n_dev,
    f_hbm,
    coef_hbm,
    rows_hbm,
    table_hbm,
    z0,
    z1,
    res_ref,
    q0,
    image_ref,
    step_z0,
    step_z1,
    step_q0,
    step_s0,
    coef_ref,
    rows_ref,
    table_ref,
    fwd_ref,
    back_ref,
    plane_ref,
    pick_ref,
    place_ref,
    u0,
    u1,
    u2,
    e0,
    e1,
    s0,
    s1,
    work,
    inv_ref,
    x1,
    y1,
    c1,
    x2,
    y2,
    c2,
    x3,
    y3,
    c3,
    x4,
    y4,
    c4,
    x5,
    y5,
    c5,
    part_a,
    part_b,
    sums_a,
    sums_b,
    near_rows,
    dots_b,
    dots_c,
    dots_d,
    load_sem,
    send_sem,
    recv_sem,
    bulk_send,
    bulk_recv,
    near_sem,
    far_sem,
):
    tabs = constants()
    weights = tabs["weights"]
    stiff = tabs["stiffness"]
    trans = tabs["transform"]
    eigen = tabs["eigen"]
    grp = lax.axis_index("grp")
    dev = lax.axis_index("dev")

    def dev_at(step):
        return lax.rem(dev + step + n_dev, n_dev)

    def grp_at(step):
        return lax.rem(grp + step + n_grp, n_grp)

    loads = [
        pltpu.make_async_copy(src, dst, load_sem.at[index])
        for index, (src, dst) in enumerate(
            (
                (f_hbm, u0),
                (table_hbm, table_ref),
                (coef_hbm, coef_ref),
                (rows_hbm, rows_ref),
            )
        )
    ]
    for load in loads:
        load.start()

    n_x = 4
    n_z = n_dev // n_x
    my_x = dev // n_z
    my_z = lax.rem(dev, n_z)

    def place_at(step_x, step_z):
        return lax.rem(my_x + step_x, n_x) * n_z + lax.rem(my_z + step_z, n_z)

    def signal(sem, where):
        pl.semaphore_signal(
            sem, inc=1, device_id=where, device_id_type=pl.DeviceIdType.MESH
        )

    barrier = pltpu.get_barrier_semaphore()
    greeted = [(grp_at(dy), dev_at(dx)) for dx, dy in SIDES]
    greeted += [(grp, place_at(0, step)) for step in range(1, n_z)]
    greeted += [(grp, place_at(step, 0)) for step in range(1, n_x)]
    greeted += [(grp_at(step), dev) for step in range(2, n_grp, 2)]
    for where in greeted:
        signal(barrier, where)

    def exchange(number, sides, source, x_ranges, y_ranges, x_buf, y_buf, c_buf):
        copies = []
        for dx, dy in sides:
            index = SIDES.index((dx, dy))
            src = source.at[
                face_range(dx, *x_ranges), face_range(dy, *y_ranges), :
            ]
            if dy == 0:
                dst = x_buf.at[0 if dx == 1 else 1]
            elif dx == 0:
                dst = y_buf.at[0 if dy == 1 else 1]
            else:
                dst = c_buf.at[0 if dx == 1 else 1, 0 if dy == 1 else 1]
            copy = pltpu.make_async_remote_copy(
                src_ref=src,
                dst_ref=dst,
                send_sem=send_sem.at[number, index],
                recv_sem=recv_sem.at[number, index],
                device_id=(grp_at(dy), dev_at(dx)),
                device_id_type=pl.DeviceIdType.MESH,
            )
            copy.start()
            copies.append(copy)
        return copies

    def arrive(copies):
        for copy in copies:
            copy.wait_recv()

    def send_row(src, dst, number, where):
        pltpu.make_async_remote_copy(
            src_ref=src,
            dst_ref=dst,
            send_sem=bulk_send.at[number],
            recv_sem=bulk_recv.at[number],
            device_id=where,
            device_id_type=pl.DeviceIdType.MESH,
        ).start()

    def from_middle(turn, count):
        half = (turn + 1) // 2
        return count // 2 + half * (1 - 2 * lax.rem(turn, 2))

    def spread_row(buf, number, along_dev):
        count = n_dev if along_dev else n_grp
        me = dev if along_dev else grp

        def body(step, carry):
            other = lax.rem(me + step, count)
            send_row(buf.at[me], buf.at[me], number, (grp, other) if along_dev else (other, dev))
            return carry

        lax.fori_loop(1, count, body, 0)

    def bulk_wait(buf, sem, count):
        part = buf.at[pl.ds(0, count)]
        pltpu.make_async_copy(part, part, sem).wait()

    low_wall = jnp.where(grp == 0, 0.0, 1.0).astype(jnp.float32)
    high_wall = jnp.where(grp == n_grp - 1, 0.0, 1.0).astype(jnp.float32)
    lane = lax.broadcasted_iota(jnp.int32, (1, LANES), 1)

    def assemble_z(ref):
        top = ref[:, pl.ds(0, NP, stride=NP), :]
        bottom = ref[:, pl.ds(NP - 1, NP, stride=NP), :]
        ref[:, pl.ds(0, NP, stride=NP), :] = top + previous_lane(bottom, 2)
        ref[:, pl.ds(NP - 1, NP, stride=NP), :] = bottom + next_lane(top, 2)

    loads[0].wait()
    assemble_z(u0)
    pl.semaphore_wait(barrier, len(greeted))
    round_1 = exchange(0, SIDES, u0, EQ_X, EQ_Y, x1, y1, c1)
    for step in range(1, n_x):
        signal(near_sem, (grp, place_at(step, 0)))
    for load in loads[1:]:
        load.wait()

    coef = coef_ref[...]
    w_k = table_ref[KROWS : KROWS + NP, :]
    half_k = table_ref[KROWS + NP : FORWARD, :]
    for ref, first in ((fwd_ref, FORWARD), (back_ref, BACK)):
        high = table_ref[first : first + KROWS, :].astype(jnp.bfloat16)
        low = table_ref[first + KROWS : first + 2 * KROWS, :].astype(jnp.bfloat16)
        ref[0:KROWS, 0:LANES] = high
        ref[0:KROWS, LANES:] = high
        ref[KROWS:, 0:LANES] = low
        ref[KROWS:, LANES:] = jnp.zeros_like(low)
    high = table_ref[PLANE : PLANE + 64, :]
    plane_ref[0:64, :] = (high + pltpu.roll(high, 64, 1)).astype(jnp.bfloat16)
    plane_ref[64:, :] = table_ref[PLANE + 64 : PLANE + 128, :].astype(jnp.bfloat16)
    place = lax.broadcasted_iota(jnp.int32, (LANES, LANES), 0)
    elem = lax.broadcasted_iota(jnp.int32, (LANES, LANES), 1)
    for index in range(3):
        block = lax.rem(dev + index + 3, 4)
        place_ref[index * LANES : (index + 1) * LANES, :] = jnp.where(
            elem == block * 32 + lax.shift_right_logical(place, 2), 1.0, 0.0
        ).astype(jnp.float32)
    for index in range(3):
        block = lax.rem(dev + index + 3, 4)
        pick_ref[:, index * LANES : (index + 1) * LANES] = jnp.where(
            place == block * 32 + lax.shift_right_logical(elem, 2), 1.0, 0.0
        ).astype(jnp.float32)
    lam_rows = table_ref[0:KROWS, :]
    for a in range(NX):
        inv_ref[a] = 1.0 / (coef * (lam_rows + eigen[a]) + MASS_SHIFT)
    pl.semaphore_wait(near_sem, n_x - 1)
    for dx, dy in ALONG_Y:
        signal(far_sem, (grp_at(dy), dev_at(dx)))
    zero_rows = jnp.zeros((128 - 80, LANES), jnp.float32)
    for i in range(NX):
        e0[i, 80:128, :] = zero_rows
        e1[i, 80:128, :] = zero_rows
        s0[i, 80:128, :] = zero_rows
        s1[i, 80:128, :] = zero_rows

    def extend_into(ext, layers, own, x_buf, y_buf, c_buf):
        for i in layers:
            if i == 0:
                row = x_buf[0, 0]
                low = c_buf[0, 0, 0]
                high = c_buf[0, 1, 0]
            elif i == NX - 1:
                row = x_buf[1, 1]
                low = c_buf[1, 0, 1]
                high = c_buf[1, 1, 1]
            else:
                row = own[i - 1]
                low = y_buf[0, i - 1]
                high = y_buf[1, i - 1]
                if i == 1:
                    row = row + x_buf[0, 1]
                    low = low + c_buf[0, 0, 1]
                    high = high + c_buf[0, 1, 1]
                elif i == NX - 2:
                    row = row + x_buf[1, 0]
                    low = low + c_buf[1, 0, 0]
                    high = high + c_buf[1, 1, 0]
            low = low * low_wall
            high = high * high_wall
            ext[i, 0:8, :] = low[0:8]
            ext[i, 8:16, :] = row[0:8] + low[8:16]
            ext[i, 16:64, :] = row[8:56]
            ext[i, 64:72, :] = row[56:64] + high[0:8]
            ext[i, 72:80, :] = high[8:16]

    def start_coarse(ext, part, sums, number):
        total = None
        for i in range(NP):
            line = combine(
                weights, [ext[i + 1, 8 + NP * j : 16 + NP * j, :] for j in range(NP)]
            )
            total = weights[i] * line if total is None else total + weights[i] * line
        total = jnp.sum(total * w_k, axis=0, keepdims=True)
        unknown = lax.broadcasted_iota(jnp.int32, (32, LANES), 0)
        elem = lax.broadcasted_iota(jnp.int32, (32, LANES), 1)
        mine = lax.shift_right_logical(elem, 2) == unknown
        column = jnp.sum(jnp.where(mine, total, 0.0), axis=1, keepdims=True)
        count = n_dev // 4
        pieces = [
            jnp.sum(rows_ref[:, m * LANES : (m + 1) * LANES] * column, axis=0, keepdims=True)
            for m in range(count)
        ]
        for m in range(count):
            first = jnp.where(lane >= 96, pieces[(m - 1) % count], pieces[m])
            last = jnp.where(lane < 32, pieces[(m + 1) % count], pieces[m])
            for index, row in enumerate((first, pieces[m], pieces[m], last)):
                part[4 * m + index] = row
        sums[1, dev] = part[dev]
        up = grp_at(1)
        down = grp_at(-1)

        def send(turn, own):
            other = place_at(from_middle(lax.rem(turn, n_x), n_x), from_middle(turn // n_x, n_z))
            send_row(part.at[other], sums.at[0, dev], number, (up, other))
            send_row(part.at[other], sums.at[2, dev], number + 2, (down, other))
            if own:
                send_row(part.at[other], sums.at[1, dev], number + 1, (grp, other))

        def body(turn, carry):
            send(turn, True)
            return carry

        lax.fori_loop(0, n_dev - 1, body, 0)
        send(n_dev - 1, False)

    def send_shares(part, sums, number):
        up = grp_at(1)
        down = grp_at(-1)

        def send(turn, own):
            other = place_at(from_middle(lax.rem(turn, n_x), n_x), from_middle(turn // n_x, n_z))
            send_row(part.at[2], sums.at[0, dev], number, (up, other))
            send_row(part.at[0], sums.at[2, dev], number + 2, (down, other))
            if own:
                send_row(part.at[1], sums.at[1, dev], number + 1, (grp, other))

        def body(turn, carry):
            send(turn, True)
            return carry

        lax.fori_loop(0, n_dev - 1, body, 0)
        send(n_dev - 1, False)

    def start_early(field, part, sums, number, dots):
        totals = []
        lines = {-1: [], 0: [], 1: []}
        for j in range(NP):
            rows = slice(NP * j, NP * j + NP)
            lines[0].append(combine(weights, [field[i, rows, :] for i in range(NP)]))
            lines[1].append(weights[0] * field[NP - 1, rows, :])
            lines[-1].append(weights[NP - 1] * field[0, rows, :])
        for step in (-1, 0, 1):
            line = lines[step]
            three = (weights[NP - 1] * line[0], combine(weights, line), weights[0] * line[NP - 1])
            totals.append(
                jnp.concatenate(
                    [jnp.sum(value * w_k, axis=0, keepdims=True) for value in three]
                    + [jnp.zeros((5, LANES), jnp.float32)],
                    axis=0,
                )
            )
        rows = jnp.dot(
            jnp.concatenate(totals, axis=1),
            place_ref[...],
            precision=HIGHEST,
            preferred_element_type=jnp.float32,
        )
        own = rows[1:2]
        free = lax.rem(dev + 2, 4) * 32
        for index, total in enumerate(dots):
            first = free + 16 * index
            row = lane_fold(jnp.sum(total, axis=0, keepdims=True))
            row = row + pltpu.roll(row, 16, 1)
            own = own + jnp.where((lane >= first) & (lane < first + 16), row, 0.0)
        part[0] = rows[0:1]
        part[1] = own
        part[2] = rows[2:3]
        sums[1, dev] = own
        send_shares(part, sums, number)

    def early_dots(sums, number):
        bulk_wait(sums.at[1], bulk_recv.at[number + 1], n_dev - 1)
        total = None
        for quarter in range(4):
            rows = [sums[1, index] for index in range(quarter, n_dev, 4)]
            row = functools.reduce(lambda a, b: a + b, rows)
            first = (quarter + 2) % 4 * 32
            row = jnp.where((lane >= first) & (lane < first + 32), row, 0.0)
            total = row if total is None else total + row
        return lane_fold(total)

    def spread_solution(sums, number):
        bulk_wait(sums.at[0], bulk_recv.at[number], n_dev)
        bulk_wait(sums.at[2], bulk_recv.at[number + 2], n_dev)
        rows = [
            sums[1, index] + (sums[0, index] * low_wall + sums[2, index] * high_wall)
            for index in range(n_dev)
        ]
        total = None
        for m in range(n_dev // 4):
            row = (
                jnp.where(lane < 64, rows[4 * m], 0.0)
                + jnp.where(lane < 96, rows[4 * m + 1], 0.0)
                + jnp.where(lane >= 32, rows[4 * m + 2], 0.0)
                + jnp.where(lane >= 64, rows[4 * m + 3], 0.0)
                + jnp.where(lane >= 96, rows[(4 * m + 4) % n_dev], 0.0)
                + jnp.where(lane < 32, rows[4 * m - 1], 0.0)
            )
            term = rows_ref[:, m * LANES : (m + 1) * LANES] * row
            total = term if total is None else total + term
        sums_q = jnp.sum(total, axis=1, keepdims=True)
        unknown = lax.broadcasted_iota(jnp.int32, (32, LANES), 0)
        elem = lax.broadcasted_iota(jnp.int32, (32, LANES), 1)
        mine = lax.shift_right_logical(elem, 2) == unknown
        near_rows[4] = jnp.sum(jnp.where(mine, sums_q, 0.0), axis=0, keepdims=True)
        for dx, dy in SIDES:
            send_row(
                near_rows.at[4],
                near_rows.at[3 * (1 - dy) + 1 - dx],
                6,
                (grp_at(dy), dev_at(dx)),
            )

    def near_lines():
        bulk_wait(near_rows, bulk_recv.at[6], 8)
        sides = []
        for index in range(3):
            sides.append(
                jnp.concatenate(
                    [near_rows[index] * low_wall, near_rows[3 + index], near_rows[6 + index] * high_wall]
                    + [jnp.zeros((5, LANES), jnp.float32)],
                    axis=0,
                )
            )
        return coarse_lines(*sides)

    def coarse_wait(sums, sem, number):
        bulk_wait(sums.at[0], sem.at[number], n_dev)
        bulk_wait(sums.at[1], sem.at[number + 1], n_dev - 1)
        bulk_wait(sums.at[2], sem.at[number + 2], n_dev)

    def finish_coarse(sums, number):
        coarse_wait(sums, bulk_recv, number)
        totals = [add_slots(sums.at[index], n_dev) for index in range(3)]
        totals = jnp.concatenate(
            [totals[0] * low_wall, totals[1], totals[2] * high_wall]
            + [jnp.zeros((5, LANES), jnp.float32)],
            axis=0,
        )
        spread = jnp.dot(
            totals, pick_ref[...], precision=HIGHEST, preferred_element_type=jnp.float32
        )
        return coarse_lines(*(spread[:, m * LANES : (m + 1) * LANES] for m in range(3)))

    def coarse_lines(before, here, after):
        node = lax.broadcasted_iota(jnp.int32, (NP, LANES), 0)
        out = []
        for value in (here + before, here, here + after):
            left = previous_lane(value, 1)
            right = next_lane(value, 1)
            lines = []
            for index in range(3):
                row = slice(index, index + 1)
                lines.append(
                    w_k
                    * (
                        value[row]
                        + jnp.where(node == 0, left[row], 0.0)
                        + jnp.where(node == NP - 1, right[row], 0.0)
                    )
                )
            out.append((lines[1] + lines[0], lines[1], lines[1] + lines[2]))
        return out

    even = [a for a in range(NX) if abs(trans[0, a] - trans[9, a]) < abs(trans[0, a] + trans[9, a])]
    odd = [a for a in range(NX) if a not in even]

    def forward(ext, pairs):
        for pair in pairs:
            parts = []
            for i in pair:
                front = previous_lane(ext[i, pl.ds(6, 16, stride=NP), :], 1)
                behind = next_lane(ext[i, pl.ds(1, 16, stride=NP), :], 1)
                parts.append(jnp.concatenate([ext[i, 0:80, :], front, behind], axis=0))
            got = dot_split(fwd_ref[...], jnp.concatenate(parts, axis=1))
            work[pair[0]] = got[:, 0:LANES]
            work[pair[1]] = got[:, LANES:]

    def solve_modes():
        def middle(block, carry):
            rows = pl.ds(pl.multiple_of(block * 8, 8), 8)
            vals = [work[i, rows, :] for i in range(NX)]
            plus = [vals[i] + vals[NX - 1 - i] for i in range(5)]
            minus = [vals[i] - vals[NX - 1 - i] for i in range(5)]
            modes = {}
            for a in range(NX):
                source = plus if a in even else minus
                modes[a] = combine(trans[:5, a], source) * inv_ref[a, rows, :]
            for i in range(5):
                sym = combine(trans[i, even], [modes[a] for a in even])
                anti = combine(trans[i, odd], [modes[a] for a in odd])
                work[i, rows, :] = sym + anti
                work[NX - 1 - i, rows, :] = sym - anti
            return carry

        lax.fori_loop(0, KROWS // 8 - 1, middle, 0)

    def backward(out, pairs):
        for pair in pairs:
            got = dot_split(
                back_ref[...], jnp.concatenate([work[pair[0]], work[pair[1]]], axis=1)
            )
            for side, i in enumerate(pair):
                part = got[:, side * LANES : (side + 1) * LANES]
                out[i, 0:80, :] = part[0:80]
                at_6 = pl.ds(6, 16, stride=NP)
                at_1 = pl.ds(1, 16, stride=NP)
                at_0 = pl.ds(0, 16, stride=NP)
                at_7 = pl.ds(7, 16, stride=NP)
                out[i, at_6, :] = out[i, at_6, :] + next_lane(part[80:96], 1)
                out[i, at_1, :] = out[i, at_1, :] + previous_lane(part[96:112], 1)
                top = out[i, at_0, :]
                bottom = out[i, at_7, :]
                out[i, at_0, :] = top + previous_lane(bottom, 1)
                out[i, at_7, :] = bottom + next_lane(top, 1)

    def extend_and_solve(arriving, ext, own, buffers, out, between):
        arrive(arriving[6:8])
        extend_into(ext, range(2, 8), own, *buffers)
        forward(ext, INNER)
        arrive(arriving[4:6])
        arrive(arriving[0:4])
        extend_into(ext, (0, 1, 8, 9), own, *buffers)
        between()
        forward(ext, OUTER)
        solve_modes()
        backward(out, OUTER)

    def send_folds(number, out, buffers):
        copies = exchange(number, CORNERS + ALONG_X, out, QF_X, QF_Y, *buffers)
        backward(out, INNER)
        return copies + exchange(number, ALONG_Y, out, QF_X, QF_Y, *buffers)

    def fold_field(out, coarse, i, x_buf, y_buf, c_buf):
        row = out[i + 1, 8:72, :]
        low = y_buf[0, i]
        high = y_buf[1, i]
        if i < 2:
            row = row + x_buf[0, i]
            low = low + c_buf[0, 0, i]
            high = high + c_buf[0, 1, i]
        elif i >= 6:
            row = row + x_buf[1, i - 6]
            low = low + c_buf[1, 0, i - 6]
            high = high + c_buf[1, 1, i - 6]
        lines = coarse[0 if i == 0 else 2 if i == NP - 1 else 1]
        terms = [
            (weights[i] * weights[j]) * lines[0 if j == 0 else 2 if j == NP - 1 else 1]
            for j in range(NP)
        ]
        return jnp.concatenate(
            [row[0:16] + low * low_wall, row[16:48], row[48:64] + high * high_wall], axis=0
        ) + jnp.concatenate(terms, axis=0)

    def operate(field, out):
        total = jnp.zeros((NP, LANES), jnp.float32)
        for pair in ((0, 7), (1, 6), (2, 5), (3, 4)):
            got = dot_split(
                plane_ref[...], jnp.concatenate([field[pair[0]], field[pair[1]]], axis=1)
            )
            out[pair[0]] = got[:, 0:LANES]
            out[pair[1]] = got[:, LANES:]
        for j in range(NP):
            rows = slice(NP * j, NP * j + NP)
            vals = [field[i, rows, :] for i in range(NP)]
            plus = [vals[i] + vals[NP - 1 - i] for i in range(4)]
            minus = [vals[i] - vals[NP - 1 - i] for i in range(4)]
            w_yz = weights[j] * w_k
            coef_yz = coef * w_yz
            for i in range(4):
                sym = combine([(stiff[i, m] + stiff[i, 7 - m]) / 2 for m in range(4)], plus)
                anti = combine([(stiff[i, m] - stiff[i, 7 - m]) / 2 for m in range(4)], minus)
                for at, value in ((i, sym + anti), (7 - i, sym - anti)):
                    result = (
                        value * coef_yz
                        + (weights[at] * coef) * out[at, rows, :]
                        + (MASS_SHIFT * weights[at]) * (w_yz * vals[at])
                    )
                    out[at, rows, :] = result
                    total = total + result * vals[at]
        return total

    def product(left, right):
        total = jnp.zeros((NP, LANES), jnp.float32)
        for j in range(NP):
            line = None
            for i in range(NP):
                term = left(i, j) * right(i, j)
                if i in (0, NP - 1):
                    term = 0.5 * term
                line = term if line is None else line + term
            if j == 0:
                line = line * (1.0 - 0.5 * low_wall)
            elif j == NP - 1:
                line = line * (1.0 - 0.5 * high_wall)
            total = total + line
        return total * half_k

    def from_ext(ext):
        return lambda i, j: ext[i + 1, 8 + NP * j : 16 + NP * j, :]

    def from_field(field):
        return lambda i, j: field[i, NP * j : NP * j + NP, :]

    def pack_dots(totals):
        packed = None
        for index, total in enumerate(totals):
            row = lane_fold(jnp.sum(total, axis=0, keepdims=True))
            mine = (lane >= 32 * index) & (lane < 32 * index + 32)
            row = jnp.where(mine, row, 0.0)
            packed = row if packed is None else packed + row
        return packed

    def unpack_dot(row, index, width):
        mine = (lane >= width * index) & (lane < width * index + width)
        return jnp.sum(jnp.where(mine, row, 0.0), axis=1, keepdims=True)

    def add_slots(buf, count):
        rows = [buf[index] for index in range(count)]
        while len(rows) > 1:
            rows = [rows[index] + rows[index + 1] for index in range(0, len(rows), 2)]
        return rows[0]

    pl.semaphore_wait(far_sem, 2)
    extend_and_solve(
        round_1, e0, u0, (x1, y1, c1), s0, lambda: start_coarse(e0, part_a, sums_a, 0)
    )
    round_2 = send_folds(1, s0, (x2, y2, c2))
    arrive(round_2)
    coarse = finish_coarse(sums_a, 0)
    for i in range(NP):
        z0[i] = fold_field(s0, coarse, i, x2, y2, c2)

    delta_part = operate(z0, u1)
    assemble_z(u1)
    round_3 = exchange(2, SIDES, u1, EQ_X, EQ_Y, x3, y3, c3)
    gamma_part = product(from_ext(e0), from_field(z0))
    start_early(u1, part_b, sums_b, 3, (gamma_part, delta_part))

    extend_and_solve(round_3, e1, u1, (x3, y3, c3), s1, lambda: None)
    round_4 = send_folds(3, s1, (x4, y4, c4))
    dots_b[grp] = early_dots(sums_b, 3)
    spread_row(dots_b, 7, False)
    spread_solution(sums_b, 3)
    for i in range(NP):
        q0[i] = e1[i + 1, 8:72, :]
    arrive(round_4)
    coarse = near_lines()
    for i in range(NP):
        z1[i] = fold_field(s1, coarse, i, x4, y4, c4)

    operate(z1, u2)
    bulk_wait(dots_b, bulk_recv.at[7], n_grp - 1)
    first_dots = add_slots(dots_b, n_grp)
    gamma_0 = unpack_dot(first_dots, 0, 16)
    delta_0 = unpack_dot(first_dots, 1, 16)
    alpha_0 = gamma_0 / delta_0
    for i in range(NP):
        z1[i] = z0[i] - alpha_0 * z1[i]
        res_ref[i] = e0[i + 1, 8:72, :] - alpha_0 * q0[i]
    gamma_part = product(from_field(res_ref), from_field(z1))
    eta_part = product(from_field(q0), from_field(z1))
    theta_part = None
    for i in range(NP):
        for j in range(NP):
            term = from_field(z1)(i, j) * from_field(u2)(i, j)
            theta_part = term if theta_part is None else theta_part + term
    dots_c[dev] = pack_dots([gamma_part, eta_part, theta_part])
    spread_row(dots_c, 8, True)
    assemble_z(u2)
    round_5 = exchange(4, SIDES, u2, Q_X, Q_Y, x5, y5, c5)
    bulk_wait(dots_c, bulk_recv.at[8], n_dev - 1)
    dots_d[grp] = add_slots(dots_c, n_dev)
    spread_row(dots_d, 9, False)
    arrive(round_5)
    for i in range(NP):
        row = u2[i]
        low = y5[0, i]
        high = y5[1, i]
        if i == 0:
            row = row + x5[0, 0]
            low = low + c5[0, 0, 0]
            high = high + c5[0, 1, 0]
        elif i == NP - 1:
            row = row + x5[1, 0]
            low = low + c5[1, 0, 0]
            high = high + c5[1, 1, 0]
        image_ref[i, 0:8, :] = row[0:8] + low * low_wall
        image_ref[i, 8:56, :] = row[8:56]
        image_ref[i, 56:64, :] = row[56:64] + high * high_wall
    bulk_wait(dots_d, bulk_recv.at[9], n_grp - 1)
    last_dots = add_slots(dots_d, n_grp)
    gamma_1 = unpack_dot(last_dots, 0, 32)
    eta = unpack_dot(last_dots, 1, 32)
    zeta = eta - alpha_0 * unpack_dot(last_dots, 2, 32)
    beta = gamma_1 / gamma_0
    alpha_1 = gamma_1 / (zeta + beta * (2.0 * eta + beta * delta_0))
    for ref, value in (
        (step_z0, alpha_0 + alpha_1 * beta),
        (step_z1, alpha_1),
        (step_q0, alpha_1 * (1.0 + beta)),
        (step_s0, -alpha_1 * alpha_0),
    ):
        ref[...] = jnp.broadcast_to(value, (1, LANES))

    for copies in (round_1, round_2, round_3, round_4, round_5):
        for copy in copies:
            copy.wait_send()
    coarse_wait(sums_a, bulk_send, 0)
    coarse_wait(sums_b, bulk_send, 3)
    for number, buf, count in (
        (6, near_rows, 9),
        (7, dots_b, n_grp),
        (8, dots_c, n_dev),
        (9, dots_d, n_grp),
    ):
        bulk_wait(buf, bulk_send.at[number], count - 1)


def local(n_grp, n_dev, forcing, coefficient, coarse_inverse):
    tabs = constants()
    field = (NP, NP * NP, LANES)
    vmem = pl.BlockSpec(memory_space=pltpu.VMEM)

    def buffers(depth):
        return [
            pltpu.VMEM((2, depth, NP * NP, LANES), jnp.float32),
            pltpu.VMEM((2, NP, NP * depth, LANES), jnp.float32),
            pltpu.VMEM((2, 2, depth, NP * depth, LANES), jnp.float32),
        ]

    ext = pltpu.VMEM((NX, 128, LANES), jnp.float32)
    full = pltpu.VMEM(field, jnp.float32)
    modes = pltpu.VMEM((NX, KROWS, LANES), jnp.float32)
    along_dev = pltpu.VMEM((n_dev, 1, LANES), jnp.float32)
    along_grp = pltpu.VMEM((n_grp, 1, LANES), jnp.float32)
    three_rows = pltpu.VMEM((3, 1, LANES), jnp.float32)
    nine_rows = pltpu.VMEM((9, 1, LANES), jnp.float32)
    three_groups = pltpu.VMEM((3, n_dev, 1, LANES), jnp.float32)
    out = jax.ShapeDtypeStruct(field, jnp.float32)
    step = jax.ShapeDtypeStruct((1, LANES), jnp.float32)
    columns = n_dev * coarse_inverse.shape[0]
    first, second, residual, first_image, second_image, *steps = pl.pallas_call(
        functools.partial(kernel, n_grp, n_dev),
        out_shape=(out,) * 5 + (step,) * 4,
        in_specs=[pl.BlockSpec(memory_space=pltpu.HBM)] * 4,
        out_specs=(vmem,) * 9,
        scratch_shapes=[
            pltpu.VMEM((1, LANES), jnp.float32),
            pltpu.VMEM(coarse_inverse[:, :columns].shape, jnp.float32),
            pltpu.VMEM((TABLE_ROWS, LANES), jnp.float32),
            pltpu.VMEM((2 * KROWS, 2 * LANES), jnp.bfloat16),
            pltpu.VMEM((2 * KROWS, 2 * LANES), jnp.bfloat16),
            pltpu.VMEM((128, LANES), jnp.bfloat16),
            pltpu.VMEM((LANES, 3 * LANES), jnp.float32),
            pltpu.VMEM((3 * LANES, LANES), jnp.float32),
            full, full, full, ext, ext, ext, ext, modes, modes,
            *buffers(2), *buffers(2), *buffers(2), *buffers(2), *buffers(1),
            along_dev, three_rows, three_groups, three_groups,
            nine_rows, along_grp, along_dev, along_grp,
            pltpu.SemaphoreType.DMA((4,)),
            pltpu.SemaphoreType.DMA((5, 8)),
            pltpu.SemaphoreType.DMA((5, 8)),
            pltpu.SemaphoreType.DMA((10,)),
            pltpu.SemaphoreType.DMA((10,)),
            pltpu.SemaphoreType.REGULAR,
            pltpu.SemaphoreType.REGULAR,
        ],
        compiler_params=pltpu.CompilerParams(
            collective_id=0, has_side_effects=True, vmem_limit_bytes=40 * 1024 * 1024
        ),
    )(
        *(
            pltpu.with_memory_space_constraint(array, pltpu.HBM)
            for array in (
                forcing.reshape(field),
                coefficient.reshape(1, LANES),
                coarse_inverse[:, :columns],
                jnp.asarray(tabs["table"]),
            )
        )
    )
    on_z0, on_z1, on_q0, on_s0 = (value.reshape(1, 1, LANES) for value in steps)
    solved = on_z0 * first + on_z1 * second
    residual = residual - (on_s0 * second_image + on_q0 * first_image)
    return solved.reshape(forcing.shape), residual.reshape(forcing.shape)


def solution(mesh):
    in_specs = (
        P(None, None, None, "dev", "grp", None),
        P("dev", "grp", None),
        P(("grp", "dev"), None),
    )
    out_specs = (P(None, None, None, "dev", "grp", None), P(None, None, None, "dev", "grp", None))
    return jax.shard_map(
        functools.partial(local, mesh.shape["grp"], mesh.shape["dev"]),
        mesh=mesh,
        in_specs=in_specs,
        out_specs=out_specs,
        check_vma=False,
    )
```

```python
import functools
import math

import jax
import jax.numpy as jnp
import ml_dtypes
import numpy as np
from jax import lax
from jax.experimental import pallas as pl
from jax.experimental.pallas import tpu as pltpu
from jax.sharding import PartitionSpec as P

NP = 8
NX = NP + 2
LANES = 128
MASS_SHIFT = 0.1
HIGHEST = lax.Precision.HIGHEST


def legendre_pair(order, point):
    before = 1.0
    current = point
    for degree in range(2, order + 1):
        before, current = (
            current,
            ((2 * degree - 1) * point * current - (degree - 1) * before) / degree,
        )
    return (before, current)


def jacobi_eigen(matrix_in):
    count = len(matrix_in)
    work = [list(row_vals) for row_vals in matrix_in]
    vectors = [
        [1.0 if row_id == col_id else 0.0 for col_id in range(count)] for row_id in range(count)
    ]
    for sweep_id in range(14):
        for first_id in range(count - 1):
            for second_id in range(first_id + 1, count):
                off_value = work[first_id][second_id]
                if abs(off_value) > 1e-300:
                    theta = (work[second_id][second_id] - work[first_id][first_id]) / (
                        2.0 * off_value
                    )
                    sign_val = 1.0 if theta >= 0.0 else -1.0
                    tangent = sign_val / (abs(theta) + math.sqrt(theta * theta + 1.0))
                    cosine = 1.0 / math.sqrt(tangent * tangent + 1.0)
                    sine = tangent * cosine
                    for other_id in range(count):
                        left_val = work[other_id][first_id]
                        right_val = work[other_id][second_id]
                        work[other_id][first_id] = cosine * left_val - sine * right_val
                        work[other_id][second_id] = sine * left_val + cosine * right_val
                    for other_id in range(count):
                        left_val = work[first_id][other_id]
                        right_val = work[second_id][other_id]
                        work[first_id][other_id] = cosine * left_val - sine * right_val
                        work[second_id][other_id] = sine * left_val + cosine * right_val
                    for other_id in range(count):
                        left_val = vectors[other_id][first_id]
                        right_val = vectors[other_id][second_id]
                        vectors[other_id][first_id] = cosine * left_val - sine * right_val
                        vectors[other_id][second_id] = sine * left_val + cosine * right_val
    return ([work[idx_val][idx_val] for idx_val in range(count)], vectors)


def element_tables(point_count):
    poly_order = point_count - 1
    points = [-math.cos(math.pi * idx_val / poly_order) for idx_val in range(point_count)]
    for newton_id in range(100):
        updated = []
        for point in points:
            before, current = legendre_pair(poly_order, point)
            updated.append(point - (point * current - before) / (point_count * current))
        points = updated
    values = [legendre_pair(poly_order, point)[1] for point in points]
    weights = [2.0 / (poly_order * point_count * value**2) for value in values]
    derivative = [[0.0] * point_count for row_id in range(point_count)]
    for left_index in range(point_count):
        for right_index in range(point_count):
            if left_index != right_index:
                derivative[left_index][right_index] = values[left_index] / (
                    values[right_index] * (points[left_index] - points[right_index])
                )
    derivative[0][0] = -poly_order * point_count / 4.0
    derivative[poly_order][poly_order] = poly_order * point_count / 4.0
    stiffness = [
        [
            sum(
                (
                    derivative[inner_id][row_id] * weights[inner_id] * derivative[inner_id][col_id]
                    for inner_id in range(point_count)
                )
            )
            for col_id in range(point_count)
        ]
        for row_id in range(point_count)
    ]
    size_three = 3 * poly_order + 1
    stiff_three = [[0.0] * size_three for row_id in range(size_three)]
    mass_three = [0.0] * size_three
    for element in range(3):
        first_node = element * poly_order
        for row_id in range(point_count):
            mass_three[first_node + row_id] += weights[row_id]
            for col_id in range(point_count):
                stiff_three[first_node + row_id][first_node + col_id] += stiffness[row_id][col_id]
    keep = list(range(poly_order - 1, 2 * poly_order + 2))
    scale_half = [1.0 / math.sqrt(mass_three[idx_val]) for idx_val in keep]
    scaled = [
        [
            scale_half[row_id] * stiff_three[keep[row_id]][keep[col_id]] * scale_half[col_id]
            for col_id in range(len(keep))
        ]
        for row_id in range(len(keep))
    ]
    eigen_values, vectors = jacobi_eigen(scaled)
    transform = [
        [scale_half[row_id] * vectors[row_id][col_id] for col_id in range(len(keep))]
        for row_id in range(len(keep))
    ]
    return (weights, stiffness, eigen_values, transform)


KROWS = 112
OUTER = ((0, 1), (8, 9))
INNER = ((2, 3), (4, 5), (6, 7))
CORNERS = ((1, 1), (1, -1), (-1, 1), (-1, -1))
ALONG_X = ((1, 0), (-1, 0))
ALONG_Y = ((0, 1), (0, -1))
SIDES = CORNERS + ALONG_X + ALONG_Y
FORWARD = 128
BACK = FORWARD + 2 * KROWS
PLANE = BACK + 2 * KROWS
TABLE_ROWS = PLANE + 2 * 64


def split_bf16(matrix):
    high = matrix.astype(ml_dtypes.bfloat16)
    low = (matrix - high.astype(np.float64)).astype(ml_dtypes.bfloat16)
    return high, low


def padded_parts(matrix):
    parts = np.zeros((2 * matrix.shape[0], LANES), np.float32)
    for index, part in enumerate(split_bf16(matrix)):
        rows = slice(index * matrix.shape[0], (index + 1) * matrix.shape[0])
        parts[rows, : matrix.shape[1]] = part.astype(np.float32)
    return parts


@functools.lru_cache(maxsize=None)
def constants():
    weights, stiffness, eigen_values, transform = (
        np.array(table, dtype=np.float64) for table in element_tables(NP)
    )
    forward = np.zeros((KROWS, KROWS))
    lam_rows = np.zeros((KROWS,))
    for b in range(NX):
        for c in range(NX):
            row = b * NX + c
            lam_rows[row] = eigen_values[b] + eigen_values[c]
            for j in range(NX):
                for k in range(NX):
                    if k == 0:
                        col = 80 + j
                    elif k == NX - 1:
                        col = 96 + j
                    else:
                        col = j * NP + k - 1
                    forward[row, col] = transform[j, b] * transform[k, c]
    diag_w = np.diag(weights)
    plane = np.kron(stiffness, diag_w) + np.kron(diag_w, stiffness)
    table = np.zeros((128, LANES), np.float32)
    table[:KROWS] = lam_rows[:, None]
    table[KROWS : KROWS + NP] = weights[:, None]
    half = np.ones((NP,))
    half[0] = half[-1] = 0.5
    table[KROWS + NP :] = half[:, None]
    return dict(
        weights=[float(v) for v in weights],
        stiffness=stiffness,
        eigen=[float(v) for v in eigen_values],
        transform=transform,
        table=np.concatenate(
            [table, padded_parts(forward), padded_parts(forward.T), padded_parts(plane)], 0
        ),
    )


def combine(scalars, vectors):
    total = None
    for scalar, vector in zip(scalars, vectors):
        term = float(scalar) * vector
        total = term if total is None else total + term
    return total


def dot_split(matrix, value):
    rows = value.shape[0]
    high = value.astype(jnp.bfloat16)
    low = (value - high.astype(jnp.float32)).astype(jnp.bfloat16)
    parts = [high, low]
    gap = matrix.shape[1] // 2 - rows
    if gap > 0:
        zeros = jnp.zeros((gap, value.shape[1]), jnp.bfloat16)
        parts = [high, zeros, low, zeros]
    out = jnp.dot(
        matrix, jnp.concatenate(parts, axis=0), preferred_element_type=jnp.float32
    )
    return out[:rows] + out[rows:]


def lane_fold(value):
    value = value + pltpu.roll(value, 64, 1)
    return value + pltpu.roll(value, 32, 1)


def next_lane(value, axis):
    return pltpu.roll(value, LANES - 1, axis)


def previous_lane(value, axis):
    return pltpu.roll(value, 1, axis)


def face_range(step, low, middle, high):
    return {1: high, -1: low, 0: middle}[step]


EQ_X = (slice(0, 2), slice(0, 8), slice(6, 8))
EQ_Y = (slice(0, 16), slice(0, 64), slice(48, 64))
QF_X = (slice(0, 2), slice(1, 9), slice(8, 10))
QF_Y = (slice(0, 16), slice(8, 72), slice(64, 80))
Q_X = (slice(0, 1), slice(0, 8), slice(7, 8))
Q_Y = (slice(0, 8), slice(0, 64), slice(56, 64))


def kernel(
    n_grp,
    n_dev,
    f_hbm,
    coef_hbm,
    rows_hbm,
    table_hbm,
    z0,
    z1,
    res_ref,
    q0,
    image_ref,
    step_z0,
    step_z1,
    step_q0,
    step_s0,
    coef_ref,
    rows_ref,
    table_ref,
    fwd_ref,
    back_ref,
    plane_ref,
    pick_ref,
    place_ref,
    u0,
    u1,
    u2,
    e0,
    e1,
    s0,
    s1,
    work,
    inv_ref,
    x1,
    y1,
    c1,
    x2,
    y2,
    c2,
    x3,
    y3,
    c3,
    x4,
    y4,
    c4,
    x5,
    y5,
    c5,
    part_a,
    part_b,
    sums_a,
    sums_b,
    near_rows,
    dots_b,
    dots_c,
    dots_d,
    load_sem,
    send_sem,
    recv_sem,
    bulk_send,
    bulk_recv,
    near_sem,
    far_sem,
):
    tabs = constants()
    weights = tabs["weights"]
    stiff = tabs["stiffness"]
    trans = tabs["transform"]
    eigen = tabs["eigen"]
    grp = lax.axis_index("grp")
    dev = lax.axis_index("dev")

    def dev_at(step):
        return lax.rem(dev + step + n_dev, n_dev)

    def grp_at(step):
        return lax.rem(grp + step + n_grp, n_grp)

    loads = [
        pltpu.make_async_copy(src, dst, load_sem.at[index])
        for index, (src, dst) in enumerate(
            (
                (f_hbm, u0),
                (table_hbm, table_ref),
                (coef_hbm, coef_ref),
                (rows_hbm, rows_ref),
            )
        )
    ]
    n_x = 4
    n_z = n_dev // n_x
    my_x = dev // n_z
    my_z = lax.rem(dev, n_z)

    def place_at(step_x, step_z):
        return lax.rem(my_x + step_x, n_x) * n_z + lax.rem(my_z + step_z, n_z)

    def signal(sem, where):
        pl.semaphore_signal(
            sem, inc=1, device_id=where, device_id_type=pl.DeviceIdType.MESH
        )

    barrier = pltpu.get_barrier_semaphore()
    greeted = [(grp_at(dy), dev_at(dx)) for dx, dy in SIDES]
    greeted += [(grp, place_at(0, step)) for step in range(1, n_z)]
    greeted += [(grp, place_at(step, 0)) for step in range(1, n_x)]
    greeted += [(grp_at(step), dev) for step in range(2, n_grp, 2)]
    for where in greeted[:8]:
        signal(barrier, where)
    for load in loads:
        load.start()
    for where in greeted[8:]:
        signal(barrier, where)

    def exchange(number, sides, source, x_ranges, y_ranges, x_buf, y_buf, c_buf):
        copies = []
        for dx, dy in sides:
            index = SIDES.index((dx, dy))
            src = source.at[
                face_range(dx, *x_ranges), face_range(dy, *y_ranges), :
            ]
            if dy == 0:
                dst = x_buf.at[0 if dx == 1 else 1]
            elif dx == 0:
                dst = y_buf.at[0 if dy == 1 else 1]
            else:
                dst = c_buf.at[0 if dx == 1 else 1, 0 if dy == 1 else 1]
            copy = pltpu.make_async_remote_copy(
                src_ref=src,
                dst_ref=dst,
                send_sem=send_sem.at[number, index],
                recv_sem=recv_sem.at[number, index],
                device_id=(grp_at(dy), dev_at(dx)),
                device_id_type=pl.DeviceIdType.MESH,
            )
            copy.start()
            copies.append(copy)
        return copies

    def arrive(copies):
        for copy in copies:
            copy.wait_recv()

    def send_row(src, dst, number, where):
        pltpu.make_async_remote_copy(
            src_ref=src,
            dst_ref=dst,
            send_sem=bulk_send.at[number],
            recv_sem=bulk_recv.at[number],
            device_id=where,
            device_id_type=pl.DeviceIdType.MESH,
        ).start()

    def from_middle(turn, count):
        half = (turn + 1) // 2
        return count // 2 + half * (1 - 2 * lax.rem(turn, 2))

    def spread_row(buf, number, along_dev):
        count = n_dev if along_dev else n_grp
        me = dev if along_dev else grp

        def body(step, carry):
            other = lax.rem(me + step, count)
            send_row(buf.at[me], buf.at[me], number, (grp, other) if along_dev else (other, dev))
            return carry

        lax.fori_loop(1, count, body, 0)

    def bulk_wait(buf, sem, count):
        part = buf.at[pl.ds(0, count)]
        pltpu.make_async_copy(part, part, sem).wait()

    low_wall = jnp.where(grp == 0, 0.0, 1.0).astype(jnp.float32)
    high_wall = jnp.where(grp == n_grp - 1, 0.0, 1.0).astype(jnp.float32)
    lane = lax.broadcasted_iota(jnp.int32, (1, LANES), 1)

    def assemble_z(ref):
        top = ref[:, pl.ds(0, NP, stride=NP), :]
        bottom = ref[:, pl.ds(NP - 1, NP, stride=NP), :]
        ref[:, pl.ds(0, NP, stride=NP), :] = top + previous_lane(bottom, 2)
        ref[:, pl.ds(NP - 1, NP, stride=NP), :] = bottom + next_lane(top, 2)

    loads[0].wait()
    assemble_z(u0)
    pl.semaphore_wait(barrier, len(greeted))
    round_1 = exchange(0, SIDES, u0, EQ_X, EQ_Y, x1, y1, c1)
    for step in range(1, n_x):
        signal(near_sem, (grp, place_at(step, 0)))
    for load in loads[1:]:
        load.wait()

    coef = coef_ref[...]
    w_k = table_ref[KROWS : KROWS + NP, :]
    half_k = table_ref[KROWS + NP : FORWARD, :]
    for ref, first in ((fwd_ref, FORWARD), (back_ref, BACK)):
        high = table_ref[first : first + KROWS, :].astype(jnp.bfloat16)
        low = table_ref[first + KROWS : first + 2 * KROWS, :].astype(jnp.bfloat16)
        ref[0:KROWS, 0:LANES] = high
        ref[0:KROWS, LANES:] = high
        ref[KROWS:, 0:LANES] = low
        ref[KROWS:, LANES:] = jnp.zeros_like(low)
    high = table_ref[PLANE : PLANE + 64, :]
    plane_ref[0:64, :] = (high + pltpu.roll(high, 64, 1)).astype(jnp.bfloat16)
    plane_ref[64:, :] = table_ref[PLANE + 64 : PLANE + 128, :].astype(jnp.bfloat16)
    place = lax.broadcasted_iota(jnp.int32, (LANES, LANES), 0)
    elem = lax.broadcasted_iota(jnp.int32, (LANES, LANES), 1)
    for index in range(3):
        block = lax.rem(dev + index + 3, 4)
        place_ref[index * LANES : (index + 1) * LANES, :] = jnp.where(
            elem == block * 32 + lax.shift_right_logical(place, 2), 1.0, 0.0
        ).astype(jnp.float32)
    for index in range(3):
        block = lax.rem(dev + index + 3, 4)
        pick_ref[:, index * LANES : (index + 1) * LANES] = jnp.where(
            place == block * 32 + lax.shift_right_logical(elem, 2), 1.0, 0.0
        ).astype(jnp.float32)
    lam_rows = table_ref[0:KROWS, :]
    for a in range(NX):
        inv_ref[a] = 1.0 / (coef * (lam_rows + eigen[a]) + MASS_SHIFT)
    pl.semaphore_wait(near_sem, n_x - 1)
    for dx, dy in ALONG_Y:
        signal(far_sem, (grp_at(dy), dev_at(dx)))
    zero_rows = jnp.zeros((128 - 80, LANES), jnp.float32)
    for i in range(NX):
        e0[i, 80:128, :] = zero_rows
        e1[i, 80:128, :] = zero_rows
        s0[i, 80:128, :] = zero_rows
        s1[i, 80:128, :] = zero_rows

    def extend_into(ext, layers, own, x_buf, y_buf, c_buf):
        for i in layers:
            if i == 0:
                row = x_buf[0, 0]
                low = c_buf[0, 0, 0]
                high = c_buf[0, 1, 0]
            elif i == NX - 1:
                row = x_buf[1, 1]
                low = c_buf[1, 0, 1]
                high = c_buf[1, 1, 1]
            else:
                row = own[i - 1]
                low = y_buf[0, i - 1]
                high = y_buf[1, i - 1]
                if i == 1:
                    row = row + x_buf[0, 1]
                    low = low + c_buf[0, 0, 1]
                    high = high + c_buf[0, 1, 1]
                elif i == NX - 2:
                    row = row + x_buf[1, 0]
                    low = low + c_buf[1, 0, 0]
                    high = high + c_buf[1, 1, 0]
            low = low * low_wall
            high = high * high_wall
            ext[i, 0:8, :] = low[0:8]
            ext[i, 8:16, :] = row[0:8] + low[8:16]
            ext[i, 16:64, :] = row[8:56]
            ext[i, 64:72, :] = row[56:64] + high[0:8]
            ext[i, 72:80, :] = high[8:16]

    def start_coarse(ext, part, sums, number):
        total = None
        for i in range(NP):
            line = combine(
                weights, [ext[i + 1, 8 + NP * j : 16 + NP * j, :] for j in range(NP)]
            )
            total = weights[i] * line if total is None else total + weights[i] * line
        total = jnp.sum(total * w_k, axis=0, keepdims=True)
        unknown = lax.broadcasted_iota(jnp.int32, (32, LANES), 0)
        elem = lax.broadcasted_iota(jnp.int32, (32, LANES), 1)
        mine = lax.shift_right_logical(elem, 2) == unknown
        column = jnp.sum(jnp.where(mine, total, 0.0), axis=1, keepdims=True)
        count = n_dev // 4
        pieces = [
            jnp.sum(rows_ref[:, m * LANES : (m + 1) * LANES] * column, axis=0, keepdims=True)
            for m in range(count)
        ]
        for m in range(count):
            first = jnp.where(lane >= 96, pieces[(m - 1) % count], pieces[m])
            last = jnp.where(lane < 32, pieces[(m + 1) % count], pieces[m])
            for index, row in enumerate((first, pieces[m], pieces[m], last)):
                part[4 * m + index] = row
        sums[1, dev] = part[dev]
        up = grp_at(1)
        down = grp_at(-1)

        def send(turn, own):
            other = place_at(from_middle(lax.rem(turn, n_x), n_x), from_middle(turn // n_x, n_z))
            send_row(part.at[other], sums.at[0, dev], number, (up, other))
            send_row(part.at[other], sums.at[2, dev], number + 2, (down, other))
            if own:
                send_row(part.at[other], sums.at[1, dev], number + 1, (grp, other))

        def body(turn, carry):
            send(turn, True)
            return carry

        lax.fori_loop(0, n_dev - 1, body, 0)
        send(n_dev - 1, False)

    def send_shares(part, sums, number):
        up = grp_at(1)
        down = grp_at(-1)

        def send(turn, own):
            other = place_at(from_middle(lax.rem(turn, n_x), n_x), from_middle(turn // n_x, n_z))
            send_row(part.at[2], sums.at[0, dev], number, (up, other))
            send_row(part.at[0], sums.at[2, dev], number + 2, (down, other))
            if own:
                send_row(part.at[1], sums.at[1, dev], number + 1, (grp, other))

        def body(turn, carry):
            send(turn, True)
            return carry

        lax.fori_loop(0, n_dev - 1, body, 0)
        send(n_dev - 1, False)

    def start_early(field, part, sums, number, dots):
        totals = []
        lines = {-1: [], 0: [], 1: []}
        for j in range(NP):
            rows = slice(NP * j, NP * j + NP)
            lines[0].append(combine(weights, [field[i, rows, :] for i in range(NP)]))
            lines[1].append(weights[0] * field[NP - 1, rows, :])
            lines[-1].append(weights[NP - 1] * field[0, rows, :])
        for step in (-1, 0, 1):
            line = lines[step]
            three = (weights[NP - 1] * line[0], combine(weights, line), weights[0] * line[NP - 1])
            totals.append(
                jnp.concatenate(
                    [jnp.sum(value * w_k, axis=0, keepdims=True) for value in three]
                    + [jnp.zeros((5, LANES), jnp.float32)],
                    axis=0,
                )
            )
        rows = jnp.dot(
            jnp.concatenate(totals, axis=1),
            place_ref[...],
            precision=HIGHEST,
            preferred_element_type=jnp.float32,
        )
        own = rows[1:2]
        free = lax.rem(dev + 2, 4) * 32
        for index, total in enumerate(dots):
            first = free + 16 * index
            row = lane_fold(jnp.sum(total, axis=0, keepdims=True))
            row = row + pltpu.roll(row, 16, 1)
            own = own + jnp.where((lane >= first) & (lane < first + 16), row, 0.0)
        part[0] = rows[0:1]
        part[1] = own
        part[2] = rows[2:3]
        sums[1, dev] = own
        send_shares(part, sums, number)

    def early_dots(sums, number):
        bulk_wait(sums.at[1], bulk_recv.at[number + 1], n_dev - 1)
        total = None
        for quarter in range(4):
            rows = [sums[1, index] for index in range(quarter, n_dev, 4)]
            row = functools.reduce(lambda a, b: a + b, rows)
            first = (quarter + 2) % 4 * 32
            row = jnp.where((lane >= first) & (lane < first + 32), row, 0.0)
            total = row if total is None else total + row
        return lane_fold(total)

    def spread_solution(sums, number):
        bulk_wait(sums.at[0], bulk_recv.at[number], n_dev)
        bulk_wait(sums.at[2], bulk_recv.at[number + 2], n_dev)
        rows = [
            sums[1, index] + (sums[0, index] * low_wall + sums[2, index] * high_wall)
            for index in range(n_dev)
        ]
        total = None
        for m in range(n_dev // 4):
            row = (
                jnp.where(lane < 64, rows[4 * m], 0.0)
                + jnp.where(lane < 96, rows[4 * m + 1], 0.0)
                + jnp.where(lane >= 32, rows[4 * m + 2], 0.0)
                + jnp.where(lane >= 64, rows[4 * m + 3], 0.0)
                + jnp.where(lane >= 96, rows[(4 * m + 4) % n_dev], 0.0)
                + jnp.where(lane < 32, rows[4 * m - 1], 0.0)
            )
            term = rows_ref[:, m * LANES : (m + 1) * LANES] * row
            total = term if total is None else total + term
        sums_q = jnp.sum(total, axis=1, keepdims=True)
        unknown = lax.broadcasted_iota(jnp.int32, (32, LANES), 0)
        elem = lax.broadcasted_iota(jnp.int32, (32, LANES), 1)
        mine = lax.shift_right_logical(elem, 2) == unknown
        near_rows[4] = jnp.sum(jnp.where(mine, sums_q, 0.0), axis=0, keepdims=True)
        for dx, dy in SIDES:
            send_row(
                near_rows.at[4],
                near_rows.at[3 * (1 - dy) + 1 - dx],
                6,
                (grp_at(dy), dev_at(dx)),
            )

    def near_lines():
        bulk_wait(near_rows, bulk_recv.at[6], 8)
        sides = []
        for index in range(3):
            sides.append(
                jnp.concatenate(
                    [near_rows[index] * low_wall, near_rows[3 + index], near_rows[6 + index] * high_wall]
                    + [jnp.zeros((5, LANES), jnp.float32)],
                    axis=0,
                )
            )
        return coarse_lines(*sides)

    def coarse_wait(sums, sem, number):
        bulk_wait(sums.at[0], sem.at[number], n_dev)
        bulk_wait(sums.at[1], sem.at[number + 1], n_dev - 1)
        bulk_wait(sums.at[2], sem.at[number + 2], n_dev)

    def finish_coarse(sums, number):
        coarse_wait(sums, bulk_recv, number)
        totals = [add_slots(sums.at[index], n_dev) for index in range(3)]
        totals = jnp.concatenate(
            [totals[0] * low_wall, totals[1], totals[2] * high_wall]
            + [jnp.zeros((5, LANES), jnp.float32)],
            axis=0,
        )
        spread = jnp.dot(
            totals, pick_ref[...], precision=HIGHEST, preferred_element_type=jnp.float32
        )
        return coarse_lines(*(spread[:, m * LANES : (m + 1) * LANES] for m in range(3)))

    def coarse_lines(before, here, after):
        node = lax.broadcasted_iota(jnp.int32, (NP, LANES), 0)
        out = []
        for value in (here + before, here, here + after):
            left = previous_lane(value, 1)
            right = next_lane(value, 1)
            lines = []
            for index in range(3):
                row = slice(index, index + 1)
                lines.append(
                    w_k
                    * (
                        value[row]
                        + jnp.where(node == 0, left[row], 0.0)
                        + jnp.where(node == NP - 1, right[row], 0.0)
                    )
                )
            out.append((lines[1] + lines[0], lines[1], lines[1] + lines[2]))
        return out

    even = [a for a in range(NX) if abs(trans[0, a] - trans[9, a]) < abs(trans[0, a] + trans[9, a])]
    odd = [a for a in range(NX) if a not in even]

    def forward(ext, pairs):
        for pair in pairs:
            parts = []
            for i in pair:
                front = previous_lane(ext[i, pl.ds(6, 16, stride=NP), :], 1)
                behind = next_lane(ext[i, pl.ds(1, 16, stride=NP), :], 1)
                parts.append(jnp.concatenate([ext[i, 0:80, :], front, behind], axis=0))
            got = dot_split(fwd_ref[...], jnp.concatenate(parts, axis=1))
            work[pair[0]] = got[:, 0:LANES]
            work[pair[1]] = got[:, LANES:]

    def solve_modes():
        def middle(block, carry):
            rows = pl.ds(pl.multiple_of(block * 8, 8), 8)
            vals = [work[i, rows, :] for i in range(NX)]
            plus = [vals[i] + vals[NX - 1 - i] for i in range(5)]
            minus = [vals[i] - vals[NX - 1 - i] for i in range(5)]
            modes = {}
            for a in range(NX):
                source = plus if a in even else minus
                modes[a] = combine(trans[:5, a], source) * inv_ref[a, rows, :]
            for i in range(5):
                sym = combine(trans[i, even], [modes[a] for a in even])
                anti = combine(trans[i, odd], [modes[a] for a in odd])
                work[i, rows, :] = sym + anti
                work[NX - 1 - i, rows, :] = sym - anti
            return carry

        lax.fori_loop(0, KROWS // 8 - 1, middle, 0)

    def backward(out, pairs):
        for pair in pairs:
            got = dot_split(
                back_ref[...], jnp.concatenate([work[pair[0]], work[pair[1]]], axis=1)
            )
            for side, i in enumerate(pair):
                part = got[:, side * LANES : (side + 1) * LANES]
                out[i, 0:80, :] = part[0:80]
                at_6 = pl.ds(6, 16, stride=NP)
                at_1 = pl.ds(1, 16, stride=NP)
                at_0 = pl.ds(0, 16, stride=NP)
                at_7 = pl.ds(7, 16, stride=NP)
                out[i, at_6, :] = out[i, at_6, :] + next_lane(part[80:96], 1)
                out[i, at_1, :] = out[i, at_1, :] + previous_lane(part[96:112], 1)
                top = out[i, at_0, :]
                bottom = out[i, at_7, :]
                out[i, at_0, :] = top + previous_lane(bottom, 1)
                out[i, at_7, :] = bottom + next_lane(top, 1)

    def extend_and_solve(arriving, ext, own, buffers, out, between):
        arrive(arriving[6:8])
        extend_into(ext, range(2, 8), own, *buffers)
        forward(ext, INNER)
        arrive(arriving[4:6])
        arrive(arriving[0:4])
        extend_into(ext, (0, 1, 8, 9), own, *buffers)
        between()
        forward(ext, OUTER)
        solve_modes()
        backward(out, OUTER)

    def send_folds(number, out, buffers):
        copies = exchange(number, CORNERS + ALONG_X, out, QF_X, QF_Y, *buffers)
        backward(out, INNER)
        return copies + exchange(number, ALONG_Y, out, QF_X, QF_Y, *buffers)

    def fold_field(out, coarse, i, x_buf, y_buf, c_buf):
        row = out[i + 1, 8:72, :]
        low = y_buf[0, i]
        high = y_buf[1, i]
        if i < 2:
            row = row + x_buf[0, i]
            low = low + c_buf[0, 0, i]
            high = high + c_buf[0, 1, i]
        elif i >= 6:
            row = row + x_buf[1, i - 6]
            low = low + c_buf[1, 0, i - 6]
            high = high + c_buf[1, 1, i - 6]
        lines = coarse[0 if i == 0 else 2 if i == NP - 1 else 1]
        terms = [
            (weights[i] * weights[j]) * lines[0 if j == 0 else 2 if j == NP - 1 else 1]
            for j in range(NP)
        ]
        return jnp.concatenate(
            [row[0:16] + low * low_wall, row[16:48], row[48:64] + high * high_wall], axis=0
        ) + jnp.concatenate(terms, axis=0)

    def operate(field, out):
        total = jnp.zeros((NP, LANES), jnp.float32)
        for pair in ((0, 7), (1, 6), (2, 5), (3, 4)):
            got = dot_split(
                plane_ref[...], jnp.concatenate([field[pair[0]], field[pair[1]]], axis=1)
            )
            out[pair[0]] = got[:, 0:LANES]
            out[pair[1]] = got[:, LANES:]
        for j in range(NP):
            rows = slice(NP * j, NP * j + NP)
            vals = [field[i, rows, :] for i in range(NP)]
            plus = [vals[i] + vals[NP - 1 - i] for i in range(4)]
            minus = [vals[i] - vals[NP - 1 - i] for i in range(4)]
            w_yz = weights[j] * w_k
            coef_yz = coef * w_yz
            for i in range(4):
                sym = combine([(stiff[i, m] + stiff[i, 7 - m]) / 2 for m in range(4)], plus)
                anti = combine([(stiff[i, m] - stiff[i, 7 - m]) / 2 for m in range(4)], minus)
                for at, value in ((i, sym + anti), (7 - i, sym - anti)):
                    result = (
                        value * coef_yz
                        + (weights[at] * coef) * out[at, rows, :]
                        + (MASS_SHIFT * weights[at]) * (w_yz * vals[at])
                    )
                    out[at, rows, :] = result
                    total = total + result * vals[at]
        return total

    def product(left, right):
        total = jnp.zeros((NP, LANES), jnp.float32)
        for j in range(NP):
            line = None
            for i in range(NP):
                term = left(i, j) * right(i, j)
                if i in (0, NP - 1):
                    term = 0.5 * term
                line = term if line is None else line + term
            if j == 0:
                line = line * (1.0 - 0.5 * low_wall)
            elif j == NP - 1:
                line = line * (1.0 - 0.5 * high_wall)
            total = total + line
        return total * half_k

    def from_ext(ext):
        return lambda i, j: ext[i + 1, 8 + NP * j : 16 + NP * j, :]

    def from_field(field):
        return lambda i, j: field[i, NP * j : NP * j + NP, :]

    def pack_dots(totals):
        packed = None
        for index, total in enumerate(totals):
            row = lane_fold(jnp.sum(total, axis=0, keepdims=True))
            mine = (lane >= 32 * index) & (lane < 32 * index + 32)
            row = jnp.where(mine, row, 0.0)
            packed = row if packed is None else packed + row
        return packed

    def unpack_dot(row, index, width):
        mine = (lane >= width * index) & (lane < width * index + width)
        return jnp.sum(jnp.where(mine, row, 0.0), axis=1, keepdims=True)

    def add_slots(buf, count):
        rows = [buf[index] for index in range(count)]
        while len(rows) > 1:
            rows = [rows[index] + rows[index + 1] for index in range(0, len(rows), 2)]
        return rows[0]

    pl.semaphore_wait(far_sem, 2)
    extend_and_solve(
        round_1, e0, u0, (x1, y1, c1), s0, lambda: start_coarse(e0, part_a, sums_a, 0)
    )
    round_2 = send_folds(1, s0, (x2, y2, c2))
    arrive(round_2)
    coarse = finish_coarse(sums_a, 0)
    for i in range(NP):
        z0[i] = fold_field(s0, coarse, i, x2, y2, c2)

    delta_part = operate(z0, u1)
    assemble_z(u1)
    round_3 = exchange(2, SIDES, u1, EQ_X, EQ_Y, x3, y3, c3)
    gamma_part = product(from_ext(e0), from_field(z0))
    start_early(u1, part_b, sums_b, 3, (gamma_part, delta_part))

    extend_and_solve(round_3, e1, u1, (x3, y3, c3), s1, lambda: None)
    round_4 = send_folds(3, s1, (x4, y4, c4))
    dots_b[grp] = early_dots(sums_b, 3)
    spread_row(dots_b, 7, False)
    spread_solution(sums_b, 3)
    for i in range(NP):
        q0[i] = e1[i + 1, 8:72, :]
    arrive(round_4)
    coarse = near_lines()
    for i in range(NP):
        z1[i] = fold_field(s1, coarse, i, x4, y4, c4)

    operate(z1, u2)
    bulk_wait(dots_b, bulk_recv.at[7], n_grp - 1)
    first_dots = add_slots(dots_b, n_grp)
    gamma_0 = unpack_dot(first_dots, 0, 16)
    delta_0 = unpack_dot(first_dots, 1, 16)
    alpha_0 = gamma_0 / delta_0
    for i in range(NP):
        z1[i] = z0[i] - alpha_0 * z1[i]
        res_ref[i] = e0[i + 1, 8:72, :] - alpha_0 * q0[i]
    gamma_part = product(from_field(res_ref), from_field(z1))
    eta_part = product(from_field(q0), from_field(z1))
    theta_part = None
    for i in range(NP):
        for j in range(NP):
            term = from_field(z1)(i, j) * from_field(u2)(i, j)
            theta_part = term if theta_part is None else theta_part + term
    dots_d[grp] = pack_dots([gamma_part, eta_part, theta_part])
    spread_row(dots_d, 9, False)
    assemble_z(u2)
    round_5 = exchange(4, SIDES, u2, Q_X, Q_Y, x5, y5, c5)
    bulk_wait(dots_d, bulk_recv.at[9], n_grp - 1)
    dots_c[dev] = add_slots(dots_d, n_grp)
    spread_row(dots_c, 8, True)
    arrive(round_5)
    for i in range(NP):
        row = u2[i]
        low = y5[0, i]
        high = y5[1, i]
        if i == 0:
            row = row + x5[0, 0]
            low = low + c5[0, 0, 0]
            high = high + c5[0, 1, 0]
        elif i == NP - 1:
            row = row + x5[1, 0]
            low = low + c5[1, 0, 0]
            high = high + c5[1, 1, 0]
        image_ref[i, 0:8, :] = row[0:8] + low * low_wall
        image_ref[i, 8:56, :] = row[8:56]
        image_ref[i, 56:64, :] = row[56:64] + high * high_wall
    bulk_wait(dots_c, bulk_recv.at[8], n_dev - 1)
    last_dots = add_slots(dots_c, n_dev)
    gamma_1 = unpack_dot(last_dots, 0, 32)
    eta = unpack_dot(last_dots, 1, 32)
    zeta = eta - alpha_0 * unpack_dot(last_dots, 2, 32)
    beta = gamma_1 / gamma_0
    alpha_1 = gamma_1 / (zeta + beta * (2.0 * eta + beta * delta_0))
    for ref, value in (
        (step_z0, alpha_0 + alpha_1 * beta),
        (step_z1, alpha_1),
        (step_q0, alpha_1 * (1.0 + beta)),
        (step_s0, -alpha_1 * alpha_0),
    ):
        ref[...] = jnp.broadcast_to(value, (1, LANES))

    for copies in (round_1, round_2, round_3, round_4, round_5):
        for copy in copies:
            copy.wait_send()
    coarse_wait(sums_a, bulk_send, 0)
    coarse_wait(sums_b, bulk_send, 3)
    for number, buf, count in (
        (6, near_rows, 9),
        (7, dots_b, n_grp),
        (8, dots_c, n_dev),
        (9, dots_d, n_grp),
    ):
        bulk_wait(buf, bulk_send.at[number], count - 1)


def local(n_grp, n_dev, forcing, coefficient, coarse_inverse):
    tabs = constants()
    field = (NP, NP * NP, LANES)
    vmem = pl.BlockSpec(memory_space=pltpu.VMEM)

    def buffers(depth):
        return [
            pltpu.VMEM((2, depth, NP * NP, LANES), jnp.float32),
            pltpu.VMEM((2, NP, NP * depth, LANES), jnp.float32),
            pltpu.VMEM((2, 2, depth, NP * depth, LANES), jnp.float32),
        ]

    ext = pltpu.VMEM((NX, 128, LANES), jnp.float32)
    full = pltpu.VMEM(field, jnp.float32)
    modes = pltpu.VMEM((NX, KROWS, LANES), jnp.float32)
    along_dev = pltpu.VMEM((n_dev, 1, LANES), jnp.float32)
    along_grp = pltpu.VMEM((n_grp, 1, LANES), jnp.float32)
    three_rows = pltpu.VMEM((3, 1, LANES), jnp.float32)
    nine_rows = pltpu.VMEM((9, 1, LANES), jnp.float32)
    three_groups = pltpu.VMEM((3, n_dev, 1, LANES), jnp.float32)
    out = jax.ShapeDtypeStruct(field, jnp.float32)
    step = jax.ShapeDtypeStruct((1, LANES), jnp.float32)
    columns = n_dev * coarse_inverse.shape[0]
    first, second, residual, first_image, second_image, *steps = pl.pallas_call(
        functools.partial(kernel, n_grp, n_dev),
        out_shape=(out,) * 5 + (step,) * 4,
        in_specs=[pl.BlockSpec(memory_space=pltpu.HBM)] * 4,
        out_specs=(vmem,) * 9,
        scratch_shapes=[
            pltpu.VMEM((1, LANES), jnp.float32),
            pltpu.VMEM(coarse_inverse[:, :columns].shape, jnp.float32),
            pltpu.VMEM((TABLE_ROWS, LANES), jnp.float32),
            pltpu.VMEM((2 * KROWS, 2 * LANES), jnp.bfloat16),
            pltpu.VMEM((2 * KROWS, 2 * LANES), jnp.bfloat16),
            pltpu.VMEM((128, LANES), jnp.bfloat16),
            pltpu.VMEM((LANES, 3 * LANES), jnp.float32),
            pltpu.VMEM((3 * LANES, LANES), jnp.float32),
            full, full, full, ext, ext, ext, ext, modes, modes,
            *buffers(2), *buffers(2), *buffers(2), *buffers(2), *buffers(1),
            along_dev, three_rows, three_groups, three_groups,
            nine_rows, along_grp, along_dev, along_grp,
            pltpu.SemaphoreType.DMA((4,)),
            pltpu.SemaphoreType.DMA((5, 8)),
            pltpu.SemaphoreType.DMA((5, 8)),
            pltpu.SemaphoreType.DMA((10,)),
            pltpu.SemaphoreType.DMA((10,)),
            pltpu.SemaphoreType.REGULAR,
            pltpu.SemaphoreType.REGULAR,
        ],
        compiler_params=pltpu.CompilerParams(
            collective_id=0, has_side_effects=True, vmem_limit_bytes=40 * 1024 * 1024
        ),
    )(
        *(
            pltpu.with_memory_space_constraint(array, pltpu.HBM)
            for array in (
                forcing.reshape(field),
                coefficient.reshape(1, LANES),
                coarse_inverse[:, :columns],
                jnp.asarray(tabs["table"]),
            )
        )
    )
    on_z0, on_z1, on_q0, on_s0 = (value.reshape(1, 1, LANES) for value in steps)
    solved = on_z0 * first + on_z1 * second
    residual = residual - (on_s0 * second_image + on_q0 * first_image)
    return solved.reshape(forcing.shape), residual.reshape(forcing.shape)


def solution(mesh):
    in_specs = (
        P(None, None, None, "dev", "grp", None),
        P("dev", "grp", None),
        P(("grp", "dev"), None),
    )
    out_specs = (P(None, None, None, "dev", "grp", None), P(None, None, None, "dev", "grp", None))
    return jax.shard_map(
        functools.partial(local, mesh.shape["grp"], mesh.shape["dev"]),
        mesh=mesh,
        in_specs=in_specs,
        out_specs=out_specs,
        check_vma=False,
    )
```

```python
import functools
import math

import jax
import jax.numpy as jnp
import ml_dtypes
import numpy as np
from jax import lax
from jax.experimental import pallas as pl
from jax.experimental.pallas import tpu as pltpu
from jax.sharding import PartitionSpec as P

NP = 8
NX = NP + 2
LANES = 128
MASS_SHIFT = 0.1
HIGHEST = lax.Precision.HIGHEST


def legendre_pair(order, point):
    before = 1.0
    current = point
    for degree in range(2, order + 1):
        before, current = (
            current,
            ((2 * degree - 1) * point * current - (degree - 1) * before) / degree,
        )
    return (before, current)


def jacobi_eigen(matrix_in):
    count = len(matrix_in)
    work = [list(row_vals) for row_vals in matrix_in]
    vectors = [
        [1.0 if row_id == col_id else 0.0 for col_id in range(count)] for row_id in range(count)
    ]
    for sweep_id in range(14):
        for first_id in range(count - 1):
            for second_id in range(first_id + 1, count):
                off_value = work[first_id][second_id]
                if abs(off_value) > 1e-300:
                    theta = (work[second_id][second_id] - work[first_id][first_id]) / (
                        2.0 * off_value
                    )
                    sign_val = 1.0 if theta >= 0.0 else -1.0
                    tangent = sign_val / (abs(theta) + math.sqrt(theta * theta + 1.0))
                    cosine = 1.0 / math.sqrt(tangent * tangent + 1.0)
                    sine = tangent * cosine
                    for other_id in range(count):
                        left_val = work[other_id][first_id]
                        right_val = work[other_id][second_id]
                        work[other_id][first_id] = cosine * left_val - sine * right_val
                        work[other_id][second_id] = sine * left_val + cosine * right_val
                    for other_id in range(count):
                        left_val = work[first_id][other_id]
                        right_val = work[second_id][other_id]
                        work[first_id][other_id] = cosine * left_val - sine * right_val
                        work[second_id][other_id] = sine * left_val + cosine * right_val
                    for other_id in range(count):
                        left_val = vectors[other_id][first_id]
                        right_val = vectors[other_id][second_id]
                        vectors[other_id][first_id] = cosine * left_val - sine * right_val
                        vectors[other_id][second_id] = sine * left_val + cosine * right_val
    return ([work[idx_val][idx_val] for idx_val in range(count)], vectors)


def element_tables(point_count):
    poly_order = point_count - 1
    points = [-math.cos(math.pi * idx_val / poly_order) for idx_val in range(point_count)]
    for newton_id in range(100):
        updated = []
        for point in points:
            before, current = legendre_pair(poly_order, point)
            updated.append(point - (point * current - before) / (point_count * current))
        points = updated
    values = [legendre_pair(poly_order, point)[1] for point in points]
    weights = [2.0 / (poly_order * point_count * value**2) for value in values]
    derivative = [[0.0] * point_count for row_id in range(point_count)]
    for left_index in range(point_count):
        for right_index in range(point_count):
            if left_index != right_index:
                derivative[left_index][right_index] = values[left_index] / (
                    values[right_index] * (points[left_index] - points[right_index])
                )
    derivative[0][0] = -poly_order * point_count / 4.0
    derivative[poly_order][poly_order] = poly_order * point_count / 4.0
    stiffness = [
        [
            sum(
                (
                    derivative[inner_id][row_id] * weights[inner_id] * derivative[inner_id][col_id]
                    for inner_id in range(point_count)
                )
            )
            for col_id in range(point_count)
        ]
        for row_id in range(point_count)
    ]
    size_three = 3 * poly_order + 1
    stiff_three = [[0.0] * size_three for row_id in range(size_three)]
    mass_three = [0.0] * size_three
    for element in range(3):
        first_node = element * poly_order
        for row_id in range(point_count):
            mass_three[first_node + row_id] += weights[row_id]
            for col_id in range(point_count):
                stiff_three[first_node + row_id][first_node + col_id] += stiffness[row_id][col_id]
    keep = list(range(poly_order - 1, 2 * poly_order + 2))
    scale_half = [1.0 / math.sqrt(mass_three[idx_val]) for idx_val in keep]
    scaled = [
        [
            scale_half[row_id] * stiff_three[keep[row_id]][keep[col_id]] * scale_half[col_id]
            for col_id in range(len(keep))
        ]
        for row_id in range(len(keep))
    ]
    eigen_values, vectors = jacobi_eigen(scaled)
    transform = [
        [scale_half[row_id] * vectors[row_id][col_id] for col_id in range(len(keep))]
        for row_id in range(len(keep))
    ]
    return (weights, stiffness, eigen_values, transform)


KROWS = 112
OUTER = ((0, 1), (8, 9))
INNER = ((2, 3), (4, 5), (6, 7))
CORNERS = ((1, 1), (1, -1), (-1, 1), (-1, -1))
ALONG_X = ((1, 0), (-1, 0))
ALONG_Y = ((0, 1), (0, -1))
SIDES = CORNERS + ALONG_X + ALONG_Y
FORWARD = 128
BACK = FORWARD + 2 * KROWS
PLANE = BACK + 2 * KROWS
TABLE_ROWS = PLANE + 2 * 64


def split_bf16(matrix):
    high = matrix.astype(ml_dtypes.bfloat16)
    low = (matrix - high.astype(np.float64)).astype(ml_dtypes.bfloat16)
    return high, low


def padded_parts(matrix):
    parts = np.zeros((2 * matrix.shape[0], LANES), np.float32)
    for index, part in enumerate(split_bf16(matrix)):
        rows = slice(index * matrix.shape[0], (index + 1) * matrix.shape[0])
        parts[rows, : matrix.shape[1]] = part.astype(np.float32)
    return parts


@functools.lru_cache(maxsize=None)
def constants():
    weights, stiffness, eigen_values, transform = (
        np.array(table, dtype=np.float64) for table in element_tables(NP)
    )
    forward = np.zeros((KROWS, KROWS))
    lam_rows = np.zeros((KROWS,))
    for b in range(NX):
        for c in range(NX):
            row = b * NX + c
            lam_rows[row] = eigen_values[b] + eigen_values[c]
            for j in range(NX):
                for k in range(NX):
                    if k == 0:
                        col = 80 + j
                    elif k == NX - 1:
                        col = 96 + j
                    else:
                        col = j * NP + k - 1
                    forward[row, col] = transform[j, b] * transform[k, c]
    diag_w = np.diag(weights)
    plane = np.kron(stiffness, diag_w) + np.kron(diag_w, stiffness)
    table = np.zeros((128, LANES), np.float32)
    table[:KROWS] = lam_rows[:, None]
    table[KROWS : KROWS + NP] = weights[:, None]
    half = np.ones((NP,))
    half[0] = half[-1] = 0.5
    table[KROWS + NP :] = half[:, None]
    return dict(
        weights=[float(v) for v in weights],
        stiffness=stiffness,
        eigen=[float(v) for v in eigen_values],
        transform=transform,
        table=np.concatenate(
            [table, padded_parts(forward), padded_parts(forward.T), padded_parts(plane)], 0
        ),
    )


def combine(scalars, vectors):
    total = None
    for scalar, vector in zip(scalars, vectors):
        term = float(scalar) * vector
        total = term if total is None else total + term
    return total


def dot_split(matrix, value):
    rows = value.shape[0]
    high = value.astype(jnp.bfloat16)
    low = (value - high.astype(jnp.float32)).astype(jnp.bfloat16)
    parts = [high, low]
    gap = matrix.shape[1] // 2 - rows
    if gap > 0:
        zeros = jnp.zeros((gap, value.shape[1]), jnp.bfloat16)
        parts = [high, zeros, low, zeros]
    out = jnp.dot(
        matrix, jnp.concatenate(parts, axis=0), preferred_element_type=jnp.float32
    )
    return out[:rows] + out[rows:]


def lane_fold(value):
    value = value + pltpu.roll(value, 64, 1)
    return value + pltpu.roll(value, 32, 1)


def next_lane(value, axis):
    return pltpu.roll(value, LANES - 1, axis)


def previous_lane(value, axis):
    return pltpu.roll(value, 1, axis)


def face_range(step, low, middle, high):
    return {1: high, -1: low, 0: middle}[step]


EQ_X = (slice(0, 2), slice(0, 8), slice(6, 8))
EQ_Y = (slice(0, 16), slice(0, 64), slice(48, 64))
QF_X = (slice(0, 2), slice(1, 9), slice(8, 10))
QF_Y = (slice(0, 16), slice(8, 72), slice(64, 80))
Q_X = (slice(0, 1), slice(0, 8), slice(7, 8))
Q_Y = (slice(0, 8), slice(0, 64), slice(56, 64))


def kernel(
    n_grp,
    n_dev,
    f_hbm,
    coef_hbm,
    rows_hbm,
    table_hbm,
    z0,
    z1,
    res_ref,
    q0,
    image_ref,
    step_z0,
    step_z1,
    step_q0,
    step_s0,
    coef_ref,
    rows_ref,
    table_ref,
    fwd_ref,
    back_ref,
    plane_ref,
    pick_ref,
    place_ref,
    u0,
    u1,
    u2,
    e0,
    e1,
    s0,
    s1,
    work,
    inv_ref,
    x1,
    y1,
    c1,
    x2,
    y2,
    c2,
    x3,
    y3,
    c3,
    x4,
    y4,
    c4,
    x5,
    y5,
    c5,
    part_a,
    part_b,
    sums_a,
    sums_b,
    near_rows,
    group_rows,
    dots_b,
    dots_c,
    dots_d,
    load_sem,
    send_sem,
    recv_sem,
    bulk_send,
    bulk_recv,
    near_sem,
    far_sem,
):
    tabs = constants()
    weights = tabs["weights"]
    stiff = tabs["stiffness"]
    trans = tabs["transform"]
    eigen = tabs["eigen"]
    grp = lax.axis_index("grp")
    dev = lax.axis_index("dev")

    def dev_at(step):
        return lax.rem(dev + step + n_dev, n_dev)

    def grp_at(step):
        return lax.rem(grp + step + n_grp, n_grp)

    loads = [
        pltpu.make_async_copy(src, dst, load_sem.at[index])
        for index, (src, dst) in enumerate(
            (
                (f_hbm, u0),
                (table_hbm, table_ref),
                (coef_hbm, coef_ref),
                (rows_hbm, rows_ref),
            )
        )
    ]
    n_x = 4
    n_z = n_dev // n_x
    my_x = dev // n_z
    my_z = lax.rem(dev, n_z)

    def place_at(step_x, step_z):
        return lax.rem(my_x + step_x, n_x) * n_z + lax.rem(my_z + step_z, n_z)

    def signal(sem, where):
        pl.semaphore_signal(
            sem, inc=1, device_id=where, device_id_type=pl.DeviceIdType.MESH
        )

    barrier = pltpu.get_barrier_semaphore()
    greeted = [(grp_at(dy), dev_at(dx)) for dx, dy in SIDES]
    greeted += [(grp, place_at(0, step)) for step in range(1, n_z)]
    greeted += [(grp, place_at(step, 0)) for step in range(1, n_x)]
    greeted += [(grp_at(step), dev) for step in range(2, n_grp, 2)]
    for where in greeted[:8]:
        signal(barrier, where)
    for load in loads:
        load.start()
    for where in greeted[8:]:
        signal(barrier, where)

    def exchange(number, sides, source, x_ranges, y_ranges, x_buf, y_buf, c_buf):
        copies = []
        for dx, dy in sides:
            index = SIDES.index((dx, dy))
            src = source.at[
                face_range(dx, *x_ranges), face_range(dy, *y_ranges), :
            ]
            if dy == 0:
                dst = x_buf.at[0 if dx == 1 else 1]
            elif dx == 0:
                dst = y_buf.at[0 if dy == 1 else 1]
            else:
                dst = c_buf.at[0 if dx == 1 else 1, 0 if dy == 1 else 1]
            copy = pltpu.make_async_remote_copy(
                src_ref=src,
                dst_ref=dst,
                send_sem=send_sem.at[number, index],
                recv_sem=recv_sem.at[number, index],
                device_id=(grp_at(dy), dev_at(dx)),
                device_id_type=pl.DeviceIdType.MESH,
            )
            copy.start()
            copies.append(copy)
        return copies

    def arrive(copies):
        for copy in copies:
            copy.wait_recv()

    def send_row(src, dst, number, where):
        pltpu.make_async_remote_copy(
            src_ref=src,
            dst_ref=dst,
            send_sem=bulk_send.at[number],
            recv_sem=bulk_recv.at[number],
            device_id=where,
            device_id_type=pl.DeviceIdType.MESH,
        ).start()

    def from_middle(turn, count):
        half = (turn + 1) // 2
        return count // 2 + half * (1 - 2 * lax.rem(turn, 2))

    def spread_row(buf, number, along_dev):
        count = n_dev if along_dev else n_grp
        me = dev if along_dev else grp

        def body(step, carry):
            other = lax.rem(me + step, count)
            send_row(buf.at[me], buf.at[me], number, (grp, other) if along_dev else (other, dev))
            return carry

        lax.fori_loop(1, count, body, 0)

    def bulk_wait(buf, sem, count):
        part = buf.at[pl.ds(0, count)]
        pltpu.make_async_copy(part, part, sem).wait()

    low_wall = jnp.where(grp == 0, 0.0, 1.0).astype(jnp.float32)
    high_wall = jnp.where(grp == n_grp - 1, 0.0, 1.0).astype(jnp.float32)
    lane = lax.broadcasted_iota(jnp.int32, (1, LANES), 1)

    def assemble_z(ref):
        top = ref[:, pl.ds(0, NP, stride=NP), :]
        bottom = ref[:, pl.ds(NP - 1, NP, stride=NP), :]
        ref[:, pl.ds(0, NP, stride=NP), :] = top + previous_lane(bottom, 2)
        ref[:, pl.ds(NP - 1, NP, stride=NP), :] = bottom + next_lane(top, 2)

    loads[0].wait()
    assemble_z(u0)
    pl.semaphore_wait(barrier, len(greeted))
    round_1 = exchange(0, SIDES, u0, EQ_X, EQ_Y, x1, y1, c1)
    for step in range(1, n_x):
        signal(near_sem, (grp, place_at(step, 0)))
    for load in loads[1:]:
        load.wait()

    coef = coef_ref[...]
    w_k = table_ref[KROWS : KROWS + NP, :]
    half_k = table_ref[KROWS + NP : FORWARD, :]
    for ref, first in ((fwd_ref, FORWARD), (back_ref, BACK)):
        high = table_ref[first : first + KROWS, :].astype(jnp.bfloat16)
        low = table_ref[first + KROWS : first + 2 * KROWS, :].astype(jnp.bfloat16)
        ref[0:KROWS, 0:LANES] = high
        ref[0:KROWS, LANES:] = high
        ref[KROWS:, 0:LANES] = low
        ref[KROWS:, LANES:] = jnp.zeros_like(low)
    high = table_ref[PLANE : PLANE + 64, :]
    plane_ref[0:64, :] = (high + pltpu.roll(high, 64, 1)).astype(jnp.bfloat16)
    plane_ref[64:, :] = table_ref[PLANE + 64 : PLANE + 128, :].astype(jnp.bfloat16)
    place = lax.broadcasted_iota(jnp.int32, (LANES, LANES), 0)
    elem = lax.broadcasted_iota(jnp.int32, (LANES, LANES), 1)
    for index in range(3):
        block = lax.rem(dev + index + 3, 4)
        place_ref[index * LANES : (index + 1) * LANES, :] = jnp.where(
            elem == block * 32 + lax.shift_right_logical(place, 2), 1.0, 0.0
        ).astype(jnp.float32)
    for index in range(3):
        block = lax.rem(dev + index + 3, 4)
        pick_ref[:, index * LANES : (index + 1) * LANES] = jnp.where(
            place == block * 32 + lax.shift_right_logical(elem, 2), 1.0, 0.0
        ).astype(jnp.float32)
    lam_rows = table_ref[0:KROWS, :]
    for a in range(NX):
        inv_ref[a] = 1.0 / (coef * (lam_rows + eigen[a]) + MASS_SHIFT)
    pl.semaphore_wait(near_sem, n_x - 1)
    for dx, dy in ALONG_Y:
        signal(far_sem, (grp_at(dy), dev_at(dx)))
    zero_rows = jnp.zeros((128 - 80, LANES), jnp.float32)
    for i in range(NX):
        e0[i, 80:128, :] = zero_rows
        e1[i, 80:128, :] = zero_rows
        s0[i, 80:128, :] = zero_rows
        s1[i, 80:128, :] = zero_rows

    def extend_into(ext, layers, own, x_buf, y_buf, c_buf):
        for i in layers:
            if i == 0:
                row = x_buf[0, 0]
                low = c_buf[0, 0, 0]
                high = c_buf[0, 1, 0]
            elif i == NX - 1:
                row = x_buf[1, 1]
                low = c_buf[1, 0, 1]
                high = c_buf[1, 1, 1]
            else:
                row = own[i - 1]
                low = y_buf[0, i - 1]
                high = y_buf[1, i - 1]
                if i == 1:
                    row = row + x_buf[0, 1]
                    low = low + c_buf[0, 0, 1]
                    high = high + c_buf[0, 1, 1]
                elif i == NX - 2:
                    row = row + x_buf[1, 0]
                    low = low + c_buf[1, 0, 0]
                    high = high + c_buf[1, 1, 0]
            low = low * low_wall
            high = high * high_wall
            ext[i, 0:8, :] = low[0:8]
            ext[i, 8:16, :] = row[0:8] + low[8:16]
            ext[i, 16:64, :] = row[8:56]
            ext[i, 64:72, :] = row[56:64] + high[0:8]
            ext[i, 72:80, :] = high[8:16]

    def start_coarse(ext, part, sums, number):
        total = None
        for i in range(NP):
            line = combine(
                weights, [ext[i + 1, 8 + NP * j : 16 + NP * j, :] for j in range(NP)]
            )
            total = weights[i] * line if total is None else total + weights[i] * line
        total = jnp.sum(total * w_k, axis=0, keepdims=True)
        unknown = lax.broadcasted_iota(jnp.int32, (32, LANES), 0)
        elem = lax.broadcasted_iota(jnp.int32, (32, LANES), 1)
        mine = lax.shift_right_logical(elem, 2) == unknown
        column = jnp.sum(jnp.where(mine, total, 0.0), axis=1, keepdims=True)
        count = n_dev // 4
        pieces = [
            jnp.sum(rows_ref[:, m * LANES : (m + 1) * LANES] * column, axis=0, keepdims=True)
            for m in range(count)
        ]
        for m in range(count):
            first = jnp.where(lane >= 96, pieces[(m - 1) % count], pieces[m])
            last = jnp.where(lane < 32, pieces[(m + 1) % count], pieces[m])
            for index, row in enumerate((first, pieces[m], pieces[m], last)):
                part[4 * m + index] = row
        sums[1, dev] = part[dev]

        def body(turn, carry):
            other = place_at(from_middle(lax.rem(turn, n_x), n_x), from_middle(turn // n_x, n_z))
            send_row(part.at[other], sums.at[1, dev], number + 1, (grp, other))
            return carry

        lax.fori_loop(0, n_dev - 1, body, 0)

    def pass_coarse(sums, number):
        bulk_wait(sums.at[1], bulk_recv.at[number + 1], n_dev - 1)
        group_rows[1] = add_slots(sums.at[1], n_dev)
        send_row(group_rows.at[1], group_rows.at[0], number, (grp_at(1), dev))
        send_row(group_rows.at[1], group_rows.at[2], number + 2, (grp_at(-1), dev))

    def send_shares(part, sums, number):
        up = grp_at(1)
        down = grp_at(-1)

        def send(turn, own):
            other = place_at(from_middle(lax.rem(turn, n_x), n_x), from_middle(turn // n_x, n_z))
            send_row(part.at[2], sums.at[0, dev], number, (up, other))
            send_row(part.at[0], sums.at[2, dev], number + 2, (down, other))
            if own:
                send_row(part.at[1], sums.at[1, dev], number + 1, (grp, other))

        def body(turn, carry):
            send(turn, True)
            return carry

        lax.fori_loop(0, n_dev - 1, body, 0)
        send(n_dev - 1, False)

    def start_early(field, part, sums, number, dots):
        totals = []
        lines = {-1: [], 0: [], 1: []}
        for j in range(NP):
            rows = slice(NP * j, NP * j + NP)
            lines[0].append(combine(weights, [field[i, rows, :] for i in range(NP)]))
            lines[1].append(weights[0] * field[NP - 1, rows, :])
            lines[-1].append(weights[NP - 1] * field[0, rows, :])
        for step in (-1, 0, 1):
            line = lines[step]
            three = (weights[NP - 1] * line[0], combine(weights, line), weights[0] * line[NP - 1])
            totals.append(
                jnp.concatenate(
                    [jnp.sum(value * w_k, axis=0, keepdims=True) for value in three]
                    + [jnp.zeros((5, LANES), jnp.float32)],
                    axis=0,
                )
            )
        rows = jnp.dot(
            jnp.concatenate(totals, axis=1),
            place_ref[...],
            precision=HIGHEST,
            preferred_element_type=jnp.float32,
        )
        own = rows[1:2]
        free = lax.rem(dev + 2, 4) * 32
        for index, total in enumerate(dots):
            first = free + 16 * index
            row = lane_fold(jnp.sum(total, axis=0, keepdims=True))
            row = row + pltpu.roll(row, 16, 1)
            own = own + jnp.where((lane >= first) & (lane < first + 16), row, 0.0)
        part[0] = rows[0:1]
        part[1] = own
        part[2] = rows[2:3]
        sums[1, dev] = own
        send_shares(part, sums, number)

    def early_dots(sums, number):
        bulk_wait(sums.at[1], bulk_recv.at[number + 1], n_dev - 1)
        total = None
        for quarter in range(4):
            rows = [sums[1, index] for index in range(quarter, n_dev, 4)]
            row = functools.reduce(lambda a, b: a + b, rows)
            first = (quarter + 2) % 4 * 32
            row = jnp.where((lane >= first) & (lane < first + 32), row, 0.0)
            total = row if total is None else total + row
        return lane_fold(total)

    def spread_solution(sums, number):
        bulk_wait(sums.at[0], bulk_recv.at[number], n_dev)
        bulk_wait(sums.at[2], bulk_recv.at[number + 2], n_dev)
        rows = [
            sums[1, index] + (sums[0, index] * low_wall + sums[2, index] * high_wall)
            for index in range(n_dev)
        ]
        total = None
        for m in range(n_dev // 4):
            row = (
                jnp.where(lane < 64, rows[4 * m], 0.0)
                + jnp.where(lane < 96, rows[4 * m + 1], 0.0)
                + jnp.where(lane >= 32, rows[4 * m + 2], 0.0)
                + jnp.where(lane >= 64, rows[4 * m + 3], 0.0)
                + jnp.where(lane >= 96, rows[(4 * m + 4) % n_dev], 0.0)
                + jnp.where(lane < 32, rows[4 * m - 1], 0.0)
            )
            term = rows_ref[:, m * LANES : (m + 1) * LANES] * row
            total = term if total is None else total + term
        sums_q = jnp.sum(total, axis=1, keepdims=True)
        unknown = lax.broadcasted_iota(jnp.int32, (32, LANES), 0)
        elem = lax.broadcasted_iota(jnp.int32, (32, LANES), 1)
        mine = lax.shift_right_logical(elem, 2) == unknown
        near_rows[4] = jnp.sum(jnp.where(mine, sums_q, 0.0), axis=0, keepdims=True)
        for dx, dy in SIDES:
            send_row(
                near_rows.at[4],
                near_rows.at[3 * (1 - dy) + 1 - dx],
                6,
                (grp_at(dy), dev_at(dx)),
            )

    def near_lines():
        bulk_wait(near_rows, bulk_recv.at[6], 8)
        sides = []
        for index in range(3):
            sides.append(
                jnp.concatenate(
                    [near_rows[index] * low_wall, near_rows[3 + index], near_rows[6 + index] * high_wall]
                    + [jnp.zeros((5, LANES), jnp.float32)],
                    axis=0,
                )
            )
        return coarse_lines(*sides)

    def coarse_wait(sums, sem, number):
        bulk_wait(sums.at[0], sem.at[number], n_dev)
        bulk_wait(sums.at[1], sem.at[number + 1], n_dev - 1)
        bulk_wait(sums.at[2], sem.at[number + 2], n_dev)

    def finish_coarse(sums, number):
        bulk_wait(group_rows, bulk_recv.at[number], 1)
        bulk_wait(group_rows, bulk_recv.at[number + 2], 1)
        totals = [group_rows[index] for index in range(3)]
        totals = jnp.concatenate(
            [totals[0] * low_wall, totals[1], totals[2] * high_wall]
            + [jnp.zeros((5, LANES), jnp.float32)],
            axis=0,
        )
        spread = jnp.dot(
            totals, pick_ref[...], precision=HIGHEST, preferred_element_type=jnp.float32
        )
        return coarse_lines(*(spread[:, m * LANES : (m + 1) * LANES] for m in range(3)))

    def coarse_lines(before, here, after):
        node = lax.broadcasted_iota(jnp.int32, (NP, LANES), 0)
        out = []
        for value in (here + before, here, here + after):
            left = previous_lane(value, 1)
            right = next_lane(value, 1)
            lines = []
            for index in range(3):
                row = slice(index, index + 1)
                lines.append(
                    w_k
                    * (
                        value[row]
                        + jnp.where(node == 0, left[row], 0.0)
                        + jnp.where(node == NP - 1, right[row], 0.0)
                    )
                )
            out.append((lines[1] + lines[0], lines[1], lines[1] + lines[2]))
        return out

    even = [a for a in range(NX) if abs(trans[0, a] - trans[9, a]) < abs(trans[0, a] + trans[9, a])]
    odd = [a for a in range(NX) if a not in even]

    def forward(ext, pairs):
        for pair in pairs:
            parts = []
            for i in pair:
                front = previous_lane(ext[i, pl.ds(6, 16, stride=NP), :], 1)
                behind = next_lane(ext[i, pl.ds(1, 16, stride=NP), :], 1)
                parts.append(jnp.concatenate([ext[i, 0:80, :], front, behind], axis=0))
            got = dot_split(fwd_ref[...], jnp.concatenate(parts, axis=1))
            work[pair[0]] = got[:, 0:LANES]
            work[pair[1]] = got[:, LANES:]

    def solve_modes():
        def middle(block, carry):
            rows = pl.ds(pl.multiple_of(block * 8, 8), 8)
            vals = [work[i, rows, :] for i in range(NX)]
            plus = [vals[i] + vals[NX - 1 - i] for i in range(5)]
            minus = [vals[i] - vals[NX - 1 - i] for i in range(5)]
            modes = {}
            for a in range(NX):
                source = plus if a in even else minus
                modes[a] = combine(trans[:5, a], source) * inv_ref[a, rows, :]
            for i in range(5):
                sym = combine(trans[i, even], [modes[a] for a in even])
                anti = combine(trans[i, odd], [modes[a] for a in odd])
                work[i, rows, :] = sym + anti
                work[NX - 1 - i, rows, :] = sym - anti
            return carry

        lax.fori_loop(0, KROWS // 8 - 1, middle, 0)

    def backward(out, pairs):
        for pair in pairs:
            got = dot_split(
                back_ref[...], jnp.concatenate([work[pair[0]], work[pair[1]]], axis=1)
            )
            for side, i in enumerate(pair):
                part = got[:, side * LANES : (side + 1) * LANES]
                out[i, 0:80, :] = part[0:80]
                at_6 = pl.ds(6, 16, stride=NP)
                at_1 = pl.ds(1, 16, stride=NP)
                at_0 = pl.ds(0, 16, stride=NP)
                at_7 = pl.ds(7, 16, stride=NP)
                out[i, at_6, :] = out[i, at_6, :] + next_lane(part[80:96], 1)
                out[i, at_1, :] = out[i, at_1, :] + previous_lane(part[96:112], 1)
                top = out[i, at_0, :]
                bottom = out[i, at_7, :]
                out[i, at_0, :] = top + previous_lane(bottom, 1)
                out[i, at_7, :] = bottom + next_lane(top, 1)

    def extend_and_solve(arriving, ext, own, buffers, out, between):
        arrive(arriving[6:8])
        extend_into(ext, range(2, 8), own, *buffers)
        forward(ext, INNER)
        arrive(arriving[4:6])
        arrive(arriving[0:4])
        extend_into(ext, (0, 1, 8, 9), own, *buffers)
        between()
        forward(ext, OUTER)
        solve_modes()
        backward(out, OUTER)

    def send_folds(number, out, buffers):
        copies = exchange(number, CORNERS + ALONG_X, out, QF_X, QF_Y, *buffers)
        backward(out, INNER)
        return copies + exchange(number, ALONG_Y, out, QF_X, QF_Y, *buffers)

    def fold_field(out, coarse, i, x_buf, y_buf, c_buf):
        row = out[i + 1, 8:72, :]
        low = y_buf[0, i]
        high = y_buf[1, i]
        if i < 2:
            row = row + x_buf[0, i]
            low = low + c_buf[0, 0, i]
            high = high + c_buf[0, 1, i]
        elif i >= 6:
            row = row + x_buf[1, i - 6]
            low = low + c_buf[1, 0, i - 6]
            high = high + c_buf[1, 1, i - 6]
        lines = coarse[0 if i == 0 else 2 if i == NP - 1 else 1]
        terms = [
            (weights[i] * weights[j]) * lines[0 if j == 0 else 2 if j == NP - 1 else 1]
            for j in range(NP)
        ]
        return jnp.concatenate(
            [row[0:16] + low * low_wall, row[16:48], row[48:64] + high * high_wall], axis=0
        ) + jnp.concatenate(terms, axis=0)

    def operate(field, out):
        total = jnp.zeros((NP, LANES), jnp.float32)
        for pair in ((0, 7), (1, 6), (2, 5), (3, 4)):
            got = dot_split(
                plane_ref[...], jnp.concatenate([field[pair[0]], field[pair[1]]], axis=1)
            )
            out[pair[0]] = got[:, 0:LANES]
            out[pair[1]] = got[:, LANES:]
        for j in range(NP):
            rows = slice(NP * j, NP * j + NP)
            vals = [field[i, rows, :] for i in range(NP)]
            plus = [vals[i] + vals[NP - 1 - i] for i in range(4)]
            minus = [vals[i] - vals[NP - 1 - i] for i in range(4)]
            w_yz = weights[j] * w_k
            coef_yz = coef * w_yz
            for i in range(4):
                sym = combine([(stiff[i, m] + stiff[i, 7 - m]) / 2 for m in range(4)], plus)
                anti = combine([(stiff[i, m] - stiff[i, 7 - m]) / 2 for m in range(4)], minus)
                for at, value in ((i, sym + anti), (7 - i, sym - anti)):
                    result = (
                        value * coef_yz
                        + (weights[at] * coef) * out[at, rows, :]
                        + (MASS_SHIFT * weights[at]) * (w_yz * vals[at])
                    )
                    out[at, rows, :] = result
                    total = total + result * vals[at]
        return total

    def product(left, right):
        total = jnp.zeros((NP, LANES), jnp.float32)
        for j in range(NP):
            line = None
            for i in range(NP):
                term = left(i, j) * right(i, j)
                if i in (0, NP - 1):
                    term = 0.5 * term
                line = term if line is None else line + term
            if j == 0:
                line = line * (1.0 - 0.5 * low_wall)
            elif j == NP - 1:
                line = line * (1.0 - 0.5 * high_wall)
            total = total + line
        return total * half_k

    def from_ext(ext):
        return lambda i, j: ext[i + 1, 8 + NP * j : 16 + NP * j, :]

    def from_field(field):
        return lambda i, j: field[i, NP * j : NP * j + NP, :]

    def pack_dots(totals):
        packed = None
        for index, total in enumerate(totals):
            row = lane_fold(jnp.sum(total, axis=0, keepdims=True))
            mine = (lane >= 32 * index) & (lane < 32 * index + 32)
            row = jnp.where(mine, row, 0.0)
            packed = row if packed is None else packed + row
        return packed

    def unpack_dot(row, index, width):
        mine = (lane >= width * index) & (lane < width * index + width)
        return jnp.sum(jnp.where(mine, row, 0.0), axis=1, keepdims=True)

    def add_slots(buf, count):
        rows = [buf[index] for index in range(count)]
        while len(rows) > 1:
            rows = [rows[index] + rows[index + 1] for index in range(0, len(rows), 2)]
        return rows[0]

    pl.semaphore_wait(far_sem, 2)
    extend_and_solve(
        round_1, e0, u0, (x1, y1, c1), s0, lambda: start_coarse(e0, part_a, sums_a, 0)
    )
    round_2 = send_folds(1, s0, (x2, y2, c2))
    pass_coarse(sums_a, 0)
    arrive(round_2)
    coarse = finish_coarse(sums_a, 0)
    for i in range(NP):
        z0[i] = fold_field(s0, coarse, i, x2, y2, c2)

    delta_part = operate(z0, u1)
    assemble_z(u1)
    round_3 = exchange(2, SIDES, u1, EQ_X, EQ_Y, x3, y3, c3)
    gamma_part = product(from_ext(e0), from_field(z0))
    start_early(u1, part_b, sums_b, 3, (gamma_part, delta_part))

    extend_and_solve(round_3, e1, u1, (x3, y3, c3), s1, lambda: None)
    round_4 = send_folds(3, s1, (x4, y4, c4))
    dots_b[grp] = early_dots(sums_b, 3)
    spread_row(dots_b, 7, False)
    spread_solution(sums_b, 3)
    for i in range(NP):
        q0[i] = e1[i + 1, 8:72, :]
    arrive(round_4)
    coarse = near_lines()
    for i in range(NP):
        z1[i] = fold_field(s1, coarse, i, x4, y4, c4)

    operate(z1, u2)
    bulk_wait(dots_b, bulk_recv.at[7], n_grp - 1)
    first_dots = add_slots(dots_b, n_grp)
    gamma_0 = unpack_dot(first_dots, 0, 16)
    delta_0 = unpack_dot(first_dots, 1, 16)
    alpha_0 = gamma_0 / delta_0
    for i in range(NP):
        z1[i] = z0[i] - alpha_0 * z1[i]
        res_ref[i] = e0[i + 1, 8:72, :] - alpha_0 * q0[i]
    gamma_part = product(from_field(res_ref), from_field(z1))
    eta_part = product(from_field(q0), from_field(z1))
    theta_part = None
    for i in range(NP):
        for j in range(NP):
            term = from_field(z1)(i, j) * from_field(u2)(i, j)
            theta_part = term if theta_part is None else theta_part + term
    dots_d[grp] = pack_dots([gamma_part, eta_part, theta_part])
    spread_row(dots_d, 9, False)
    assemble_z(u2)
    round_5 = exchange(4, SIDES, u2, Q_X, Q_Y, x5, y5, c5)
    bulk_wait(dots_d, bulk_recv.at[9], n_grp - 1)
    dots_c[dev] = add_slots(dots_d, n_grp)
    spread_row(dots_c, 8, True)
    arrive(round_5)
    for i in range(NP):
        row = u2[i]
        low = y5[0, i]
        high = y5[1, i]
        if i == 0:
            row = row + x5[0, 0]
            low = low + c5[0, 0, 0]
            high = high + c5[0, 1, 0]
        elif i == NP - 1:
            row = row + x5[1, 0]
            low = low + c5[1, 0, 0]
            high = high + c5[1, 1, 0]
        image_ref[i, 0:8, :] = row[0:8] + low * low_wall
        image_ref[i, 8:56, :] = row[8:56]
        image_ref[i, 56:64, :] = row[56:64] + high * high_wall
    bulk_wait(dots_c, bulk_recv.at[8], n_dev - 1)
    last_dots = add_slots(dots_c, n_dev)
    gamma_1 = unpack_dot(last_dots, 0, 32)
    eta = unpack_dot(last_dots, 1, 32)
    zeta = eta - alpha_0 * unpack_dot(last_dots, 2, 32)
    beta = gamma_1 / gamma_0
    alpha_1 = gamma_1 / (zeta + beta * (2.0 * eta + beta * delta_0))
    for ref, value in (
        (step_z0, alpha_0 + alpha_1 * beta),
        (step_z1, alpha_1),
        (step_q0, alpha_1 * (1.0 + beta)),
        (step_s0, -alpha_1 * alpha_0),
    ):
        ref[...] = jnp.broadcast_to(value, (1, LANES))

    for copies in (round_1, round_2, round_3, round_4, round_5):
        for copy in copies:
            copy.wait_send()
    bulk_wait(group_rows, bulk_send.at[0], 1)
    bulk_wait(sums_a.at[1], bulk_send.at[1], n_dev - 1)
    bulk_wait(group_rows, bulk_send.at[2], 1)
    coarse_wait(sums_b, bulk_send, 3)
    for number, buf, count in (
        (6, near_rows, 9),
        (7, dots_b, n_grp),
        (8, dots_c, n_dev),
        (9, dots_d, n_grp),
    ):
        bulk_wait(buf, bulk_send.at[number], count - 1)


def local(n_grp, n_dev, forcing, coefficient, coarse_inverse):
    tabs = constants()
    field = (NP, NP * NP, LANES)
    vmem = pl.BlockSpec(memory_space=pltpu.VMEM)

    def buffers(depth):
        return [
            pltpu.VMEM((2, depth, NP * NP, LANES), jnp.float32),
            pltpu.VMEM((2, NP, NP * depth, LANES), jnp.float32),
            pltpu.VMEM((2, 2, depth, NP * depth, LANES), jnp.float32),
        ]

    ext = pltpu.VMEM((NX, 128, LANES), jnp.float32)
    full = pltpu.VMEM(field, jnp.float32)
    modes = pltpu.VMEM((NX, KROWS, LANES), jnp.float32)
    along_dev = pltpu.VMEM((n_dev, 1, LANES), jnp.float32)
    along_grp = pltpu.VMEM((n_grp, 1, LANES), jnp.float32)
    three_rows = pltpu.VMEM((3, 1, LANES), jnp.float32)
    nine_rows = pltpu.VMEM((9, 1, LANES), jnp.float32)
    three_groups = pltpu.VMEM((3, n_dev, 1, LANES), jnp.float32)
    out = jax.ShapeDtypeStruct(field, jnp.float32)
    step = jax.ShapeDtypeStruct((1, LANES), jnp.float32)
    columns = n_dev * coarse_inverse.shape[0]
    first, second, residual, first_image, second_image, *steps = pl.pallas_call(
        functools.partial(kernel, n_grp, n_dev),
        out_shape=(out,) * 5 + (step,) * 4,
        in_specs=[pl.BlockSpec(memory_space=pltpu.HBM)] * 4,
        out_specs=(vmem,) * 9,
        scratch_shapes=[
            pltpu.VMEM((1, LANES), jnp.float32),
            pltpu.VMEM(coarse_inverse[:, :columns].shape, jnp.float32),
            pltpu.VMEM((TABLE_ROWS, LANES), jnp.float32),
            pltpu.VMEM((2 * KROWS, 2 * LANES), jnp.bfloat16),
            pltpu.VMEM((2 * KROWS, 2 * LANES), jnp.bfloat16),
            pltpu.VMEM((128, LANES), jnp.bfloat16),
            pltpu.VMEM((LANES, 3 * LANES), jnp.float32),
            pltpu.VMEM((3 * LANES, LANES), jnp.float32),
            full, full, full, ext, ext, ext, ext, modes, modes,
            *buffers(2), *buffers(2), *buffers(2), *buffers(2), *buffers(1),
            along_dev, three_rows, three_groups, three_groups,
            nine_rows, three_rows, along_grp, along_dev, along_grp,
            pltpu.SemaphoreType.DMA((4,)),
            pltpu.SemaphoreType.DMA((5, 8)),
            pltpu.SemaphoreType.DMA((5, 8)),
            pltpu.SemaphoreType.DMA((10,)),
            pltpu.SemaphoreType.DMA((10,)),
            pltpu.SemaphoreType.REGULAR,
            pltpu.SemaphoreType.REGULAR,
        ],
        compiler_params=pltpu.CompilerParams(
            collective_id=0, has_side_effects=True, vmem_limit_bytes=40 * 1024 * 1024
        ),
    )(
        *(
            pltpu.with_memory_space_constraint(array, pltpu.HBM)
            for array in (
                forcing.reshape(field),
                coefficient.reshape(1, LANES),
                coarse_inverse[:, :columns],
                jnp.asarray(tabs["table"]),
            )
        )
    )
    on_z0, on_z1, on_q0, on_s0 = (value.reshape(1, 1, LANES) for value in steps)
    solved = on_z0 * first + on_z1 * second
    residual = residual - (on_s0 * second_image + on_q0 * first_image)
    return solved.reshape(forcing.shape), residual.reshape(forcing.shape)


def solution(mesh):
    in_specs = (
        P(None, None, None, "dev", "grp", None),
        P("dev", "grp", None),
        P(("grp", "dev"), None),
    )
    out_specs = (P(None, None, None, "dev", "grp", None), P(None, None, None, "dev", "grp", None))
    return jax.shard_map(
        functools.partial(local, mesh.shape["grp"], mesh.shape["dev"]),
        mesh=mesh,
        in_specs=in_specs,
        out_specs=out_specs,
        check_vma=False,
    )
```
